256 devices in a mesh: dp: 16 (over x, z_lo, core), sh: 4 (over z_hi), sw: 4 (over y).
Axes of the slice: x: 4, y: 4, z: 8 (z_hi: 4, z_lo: 2; z = z_hi * 2 + z_lo), core: 2. Of those that a mesh axis runs over, the one named last changes fastest.
Arguments:
- query_tokens: bfloat16 [16, 2, 32, 32, 1536], P('dp', None, 'sh', 'sw'), may hold values from -18 to 18
- key_tokens: bfloat16 [16, 2, 32, 32, 1536], P('dp', None, 'sh', 'sw'), may hold values from -18 to 18
- value_tokens: bfloat16 [16, 2, 32, 32, 1536], P('dp', None, 'sh', 'sw'), may hold values from -24 to 24
- window_first_tile: int32 [2, 4, 4], replicated, may hold values from 0 to 1, as said below
- output_weight_matrix: bfloat16 [1536, 1536], P(None, 'dp'), may hold values from -0.15625 to 0.15625
- adapter_down_weight: bfloat16 [1536, 64], replicated, may hold values from -0.15625 to 0.15625
- adapter_up_weight: bfloat16 [64, 1536], replicated, may hold values from -0.75 to 0.75
- output_gradient: bfloat16 [16, 2, 32, 32, 1536], P('dp', None, 'sh', 'sw'), may hold values from -6 to 6
Outputs:
- output: bfloat16 [16, 2, 32, 32, 1536], P('dp', None, 'sh', 'sw')
- query_grad: bfloat16 [16, 2, 32, 32, 1536], P('dp', None, 'sh', 'sw')
- key_grad: bfloat16 [16, 2, 32, 32, 1536], P('dp', None, 'sh', 'sw')
- value_grad: bfloat16 [16, 2, 32, 32, 1536], P('dp', None, 'sh', 'sw')
- down_grad: float32 [1536, 64], replicated
- up_weight_gradient: float32 [64, 1536], replicated
The draws below stay inside these ranges and needn't reach their ends.
Inputs may be any that keep to these rules, and one draw needn't show every extreme that they name: window_first_tile[0, i, j] lies between max(0, i - 2) and min(i, 1); window_first_tile[1, i, j] between max(0, j - 2) and min(j, 1).
All inputs are finite; a program needn't handle non-finite values.
Results may differ from the reference program's by a relative error of at most 0.024.
Values may be sent and summed in bfloat16 or wider, within the bound.
A program may use at most 128 MiB of HBM per device.

```python
import jax
import jax.numpy as jnp
from jax import lax

HEADS = 12
HEAD = 128
OUTPUT_HALF = 1536
ADAPTER_RANK = 64
FRAMES = 2
TILE_H = 8
TILE_W = 8
WINDOW = 3
HEAD_FEATURES = 1536
BATCH = 16
LAT_H = 32
LAT_W = 32
TILES_H = 4
TILES_W = 4
TOKENS = 32768


def draw_query_tokens(key, part):
    key = jax.random.fold_in(key, 11)
    base_key = jax.random.fold_in(key, 0)
    full_shape = (BATCH, FRAMES, LAT_H, LAT_W, HEAD_FEATURES)
    base_part = jnp.clip(1.4 * jax.random.normal(base_key, full_shape, jnp.float32), -8.0, 8.0)
    return base_part.astype(jnp.bfloat16)


def draw_key_tokens(key, part):
    key = jax.random.fold_in(key, 12)
    base_key = jax.random.fold_in(key, 0)
    full_shape = (BATCH, FRAMES, LAT_H, LAT_W, HEAD_FEATURES)
    base_part = jnp.clip(1.4 * jax.random.normal(base_key, full_shape, jnp.float32), -8.0, 8.0)
    return base_part.astype(jnp.bfloat16)


def draw_window_first_tile(key, part):
    key = jax.random.fold_in(key, 13)
    row_index = jnp.broadcast_to(jnp.arange(TILES_H, dtype=jnp.int32)[:, None], (TILES_H, TILES_W))
    col_index = jnp.broadcast_to(jnp.arange(TILES_W, dtype=jnp.int32)[None, :], (TILES_H, TILES_W))
    step_back = jax.random.randint(key, (2, TILES_H, TILES_W), 0, 3, dtype=jnp.int32)
    row_begin = jnp.clip(row_index - step_back[0], 0, TILES_H - WINDOW)
    col_begin = jnp.clip(col_index - step_back[1], 0, TILES_W - WINDOW)
    return jnp.stack([row_begin, col_begin], axis=0).astype(jnp.int32)


def steps_of(own_key, extent, cuts, smallest, high):
    def one(dim, parts):
        draws = jax.random.uniform(jax.random.fold_in(jax.random.fold_in(own_key, 6), dim), (parts,), jnp.float32, smallest / len(cuts), high / len(cuts))
        return jnp.repeat(jnp.exp(draws), extent[dim] // parts).reshape((-1,) + (1,) * (len(extent) - dim - 1))

    gain = one(*cuts[0])
    for cut in cuts[1:]:
        gain = gain * one(*cut)
    return gain


def noise(key, shape, deviation, limit, cuts=(), kind=jnp.bfloat16):
    values = deviation * jax.random.normal(key, shape, jnp.float32)
    if cuts:
        values = values * steps_of(key, shape, cuts, -0.22, 0.18)
    return jnp.clip(values, -limit, limit).astype(kind)


def setup_inputs(seed: int = 0) -> dict:
    keys = jax.random.split(jax.random.key(seed), 9)
    return {
        "query_tokens": draw_query_tokens(jax.random.fold_in(keys[8], 71), 0),
        "key_tokens": draw_key_tokens(jax.random.fold_in(keys[8], 71), 0),
        "value_tokens": noise(keys[2], (BATCH, FRAMES, LAT_H, LAT_W, HEAD_FEATURES), 4.0, 24.0, ((0, 16), (2, 4), (3, 4))),
        "window_first_tile": draw_window_first_tile(jax.random.fold_in(keys[8], 71), 0),
        "output_weight_matrix": noise(keys[4], (HEAD_FEATURES, OUTPUT_HALF), HEAD_FEATURES ** -0.5, 0.15625, ((1, 16),)),
        "adapter_down_weight": noise(keys[5], (HEAD_FEATURES, ADAPTER_RANK), HEAD_FEATURES ** -0.5, 0.15625),
        "adapter_up_weight": noise(keys[6], (ADAPTER_RANK, OUTPUT_HALF), ADAPTER_RANK ** -0.5, 0.75),
        "output_gradient": noise(keys[7], (BATCH, FRAMES, LAT_H, LAT_W, OUTPUT_HALF), 1.0, 6.0, ((0, 16), (2, 4), (3, 4))),
    }


def split_heads(array):
    return array.reshape(array.shape[0], -1, HEADS, HEAD).astype(jnp.float32)


def tile_of(array, row_tile, col_tile):
    return array[:, :, row_tile * TILE_H:(row_tile + 1) * TILE_H, col_tile * TILE_W:(col_tile + 1) * TILE_W, :]


def window_index(row_begin, col_begin):
    zero = jnp.zeros((), jnp.int32)
    return (zero, zero, (row_begin * TILE_H).astype(jnp.int32), (col_begin * TILE_W).astype(jnp.int32), zero)


def window_of(array, row_begin, col_begin):
    sizes = (array.shape[0], array.shape[1], WINDOW * TILE_H, WINDOW * TILE_W, array.shape[4])
    return lax.dynamic_slice(array, window_index(row_begin, col_begin), sizes)


def add_window(accum, term, row_begin, col_begin):
    current = window_of(accum, row_begin, col_begin)
    return lax.dynamic_update_slice(accum, current + term, window_index(row_begin, col_begin))


def tile_weights(query_heads, key_heads, factor):
    scores = jnp.einsum("bqhd,bkhd->bhqk", query_heads, key_heads) * factor
    row_top = jnp.max(scores, axis=-1, keepdims=True)
    exponent = jnp.exp(scores - row_top)
    return (exponent / jnp.sum(exponent, axis=-1, keepdims=True)).astype(jnp.bfloat16)


def reference(query_tokens, key_tokens, value_tokens, window_first_tile, output_weight_matrix, adapter_down_weight, adapter_up_weight, output_gradient):
    factor = HEAD ** -0.5
    tile_shape = (BATCH, FRAMES, TILE_H, TILE_W, HEAD_FEATURES)
    window_shape = (BATCH, FRAMES, WINDOW * TILE_H, WINDOW * TILE_W, HEAD_FEATURES)
    rows_out = []
    for row_tile in range(TILES_H):
        cols_out = []
        for col_tile in range(TILES_W):
            row_begin = window_first_tile[0, row_tile, col_tile]
            col_begin = window_first_tile[1, row_tile, col_tile]
            query_heads = split_heads(tile_of(query_tokens, row_tile, col_tile))
            key_heads = split_heads(window_of(key_tokens, row_begin, col_begin))
            value_heads = split_heads(window_of(value_tokens, row_begin, col_begin))
            weights = tile_weights(query_heads, key_heads, factor)
            attended_tile = jnp.einsum("bhqk,bkhd->bqhd", weights.astype(jnp.float32), value_heads)
            cols_out.append(attended_tile.astype(jnp.bfloat16).reshape(tile_shape))
        rows_out.append(jnp.concatenate(cols_out, axis=3))
    attended = jnp.concatenate(rows_out, axis=2)

    flattened_attention = attended.reshape(-1, HEAD_FEATURES)
    flattened_gradient = output_gradient.reshape(-1, OUTPUT_HALF)
    adapter_middle = jnp.dot(flattened_attention, adapter_down_weight, preferred_element_type=jnp.float32).astype(jnp.bfloat16)
    output = (jnp.dot(flattened_attention, output_weight_matrix, preferred_element_type=jnp.float32)
              + jnp.dot(adapter_middle, adapter_up_weight, preferred_element_type=jnp.float32)).astype(jnp.bfloat16)
    output = output.reshape(output_gradient.shape)
    middle_gradient = jnp.dot(flattened_gradient, adapter_up_weight.T, preferred_element_type=jnp.float32).astype(jnp.bfloat16)
    attended_grad = (jnp.dot(flattened_gradient, output_weight_matrix.T, preferred_element_type=jnp.float32)
                     + jnp.dot(middle_gradient, adapter_down_weight.T, preferred_element_type=jnp.float32)).astype(jnp.bfloat16)
    attended_grad = attended_grad.reshape(attended.shape)
    gradient_norm = TOKENS ** -0.5
    down_grad = jnp.dot(flattened_attention.T, middle_gradient, preferred_element_type=jnp.float32) * gradient_norm
    up_weight_gradient = jnp.dot(adapter_middle.T, flattened_gradient, preferred_element_type=jnp.float32) * gradient_norm

    key_accum = jnp.zeros(key_tokens.shape, jnp.float32)
    value_accum = jnp.zeros(value_tokens.shape, jnp.float32)
    rows_out = []
    for row_tile in range(TILES_H):
        cols_out = []
        for col_tile in range(TILES_W):
            row_begin = window_first_tile[0, row_tile, col_tile]
            col_begin = window_first_tile[1, row_tile, col_tile]
            query_heads = split_heads(tile_of(query_tokens, row_tile, col_tile))
            key_heads = split_heads(window_of(key_tokens, row_begin, col_begin))
            value_heads = split_heads(window_of(value_tokens, row_begin, col_begin))
            grad_heads = split_heads(tile_of(attended_grad, row_tile, col_tile))
            weights = tile_weights(query_heads, key_heads, factor).astype(jnp.float32)
            prob_grad = jnp.einsum("bqhd,bkhd->bhqk", grad_heads, value_heads)
            row_delta = jnp.sum(weights * prob_grad, axis=-1, keepdims=True)
            score_grad = (weights * (prob_grad - row_delta) * factor).astype(jnp.bfloat16).astype(jnp.float32)
            query_part = jnp.einsum("bhqk,bkhd->bqhd", score_grad, key_heads)
            cols_out.append(query_part.astype(jnp.bfloat16).reshape(tile_shape))
            key_term = jnp.einsum("bhqk,bqhd->bkhd", score_grad, query_heads).astype(jnp.bfloat16)
            value_term = jnp.einsum("bhqk,bqhd->bkhd", weights, grad_heads).astype(jnp.bfloat16)
            key_term = lax.optimization_barrier(key_term).astype(jnp.float32).reshape(window_shape)
            value_term = lax.optimization_barrier(value_term).astype(jnp.float32).reshape(window_shape)
            key_accum = add_window(key_accum, key_term, row_begin, col_begin)
            value_accum = add_window(value_accum, value_term, row_begin, col_begin)
        rows_out.append(jnp.concatenate(cols_out, axis=3))
    query_grad = jnp.concatenate(rows_out, axis=2)
    return (output, query_grad, key_accum.astype(jnp.bfloat16), value_accum.astype(jnp.bfloat16), down_grad, up_weight_gradient)
```

```python
import functools

import jax
import jax.numpy as jnp
from jax import lax
from jax.experimental import pallas as pl
from jax.experimental.pallas import tpu as pltpu
from jax.sharding import PartitionSpec as P

MESH = pl.DeviceIdType.MESH
HEADS = 12
HEAD = 128
WINDOW = 3
GROUP = 3
GRID = 4
TOK = 128
RANK = 64
FEAT = 1536
SPAN = GROUP * HEAD
SHARD = 96
TOKENS = 32768
BF = jnp.bfloat16
F32 = jnp.float32
NT = (((1,), (1,)), ((), ()))
TN = (((0,), (0,)), ((), ()))
NN = (((1,), (0,)), ((), ()))


def dot(a, b, dims):
    return lax.dot_general(a, b, dims, preferred_element_type=F32)


class Sems:
    def __init__(self, send, recv):
        self.send, self.recv, self.used = send, recv, 0

    def copy(self, src, dst, device):
        slot = self.used
        self.used += 1
        made = pltpu.make_async_remote_copy(
            src_ref=src,
            dst_ref=dst,
            send_sem=self.send.at[slot],
            recv_sem=self.recv.at[slot],
            device_id=device,
            device_id_type=MESH,
        )
        made.start()
        return made


def place():
    return lax.axis_index("dp"), lax.axis_index("sh"), lax.axis_index("sw")


def turn(index, by, size):
    return lax.rem(index + by, size)


def flip(dp, bit):
    return dp + bit - 2 * bit * lax.rem(lax.div(dp, bit), 2)


def greet(devices):
    barrier = pltpu.get_barrier_semaphore()
    for device in devices:
        pl.semaphore_signal(barrier, inc=1, device_id=device, device_id_type=MESH)
    pl.semaphore_wait(barrier, len(devices))


SPREAD_COPIES = 9 + 24 + 15 + 3


def spread_kernel(
    q_ref, k_ref, v_ref, og_ref, w_ref, down_ref, up_ref,
    qz, kall, vall, doz, wt, midg,
    qs, ks, vs, dos, send, recv,
):
    dp, sh, sw = place()
    sems = Sems(send, recv)
    row_peer = [(dp, turn(sh, d, GRID), sw) for d in (1, 2, 3)]
    col_peer = [(dp, sh, turn(sw, d, GRID)) for d in (1, 2, 3)]
    x_peer = [(turn(dp, 4 * d, 16), sh, sw) for d in (1, 2, 3)]
    zlo = (flip(dp, 2), sh, sw)
    twin = (flip(dp, 1), sh, sw)
    for h in range(HEADS):
        cols = slice(h * HEAD, (h + 1) * HEAD)
        ks[h] = k_ref[:, cols]
        vs[h] = v_ref[:, cols]
        qs[h] = q_ref[:, cols]
    for j in range(GROUP):
        kall[j, sw, sh] = ks[sh * GROUP + j]
        vall[j, sw, sh] = vs[sh * GROUP + j]
        qz[j, sh] = qs[sh * GROUP + j]
    own_rows = pl.ds(pl.multiple_of(dp * SHARD, SHARD), SHARD)
    wt[own_rows, :] = w_ref[...]
    greet(row_peer + col_peer + x_peer + [zlo, twin])

    pending = []

    def rows_to(stack, peer):
        return stack.at[pl.ds(peer[1] * GROUP, GROUP)]

    k_in, v_in, q_in = [], [], []
    for peer in row_peer:
        k_in.append(sems.copy(rows_to(ks, peer), kall.at[:, sw, sh], peer))
        v_in.append(sems.copy(rows_to(vs, peer), vall.at[:, sw, sh], peer))

    def shard_of(owner):
        return wt.at[pl.ds(pl.multiple_of(owner * SHARD, SHARD), SHARD)]

    def pass_on(owner, peer):
        return sems.copy(shard_of(owner), shard_of(owner), peer)

    zlo_in = pass_on(dp, zlo)
    own_in = [pass_on(dp, peer) for peer in x_peer]
    twin_in = [pass_on(dp, twin)]

    def down_the_row(row):
        for stack in (kall, vall):
            for peer in col_peer:
                block = stack.at[:, sw, row]
                pending.append(sems.copy(block, block, peer))

    down_the_row(sh)
    for peer in row_peer:
        q_in.append(sems.copy(rows_to(qs, peer), qz.at[:, sh], peer))

    mid = dot(og_ref[...], up_ref[...], NT).astype(BF)
    midg[...] = mid

    zlo_in.wait_recv()
    other_in = [pass_on(flip(dp, 2), peer) for peer in x_peer]
    twin_in.append(pass_on(flip(dp, 2), twin))
    for d in (0, 2, 1):
        k_in[d].wait_recv()
        v_in[d].wait_recv()
        down_the_row(turn(sh, GRID - d - 1, GRID))
    for d in (0, 2, 1):
        owner = turn(dp, 16 - 4 * (d + 1), 16)
        own_in[d].wait_recv()
        twin_in.append(pass_on(owner, twin))
        other_in[d].wait_recv()
        twin_in.append(pass_on(flip(owner, 2), twin))
    for made in twin_in:
        made.wait_recv()

    do_in = []
    for d in (1, 3, 2, 0):
        target = turn(sh, d, GRID)
        cols = pl.ds(pl.multiple_of(target * SPAN, HEAD), SPAN)
        part = dot(og_ref[...], wt[:, cols], NN) + dot(midg[...], down_ref[:, cols], NN)
        part = part.astype(BF)
        for j in range(GROUP):
            piece = part[:, j * HEAD : (j + 1) * HEAD]
            if d:
                dos[target * GROUP + j] = piece
            else:
                doz[j, sh] = piece
        if d:
            peer = (dp, target, sw)
            do_in.append(sems.copy(rows_to(dos, peer), doz.at[:, sh], peer))
    for made in k_in + v_in + own_in + other_in + twin_in + [zlo_in]:
        made.wait_send()
    for made in q_in + do_in + pending:
        made.wait()


def attend_kernel(table, qz, doz, kall, vall, o_out, dq_out, dk_out, dv_out, dk, dv):
    factor = HEAD ** (-0.5)
    dk[...] = jnp.zeros_like(dk)
    dv[...] = jnp.zeros_like(dv)

    def unit(step, carry):
        j = step // GRID
        i = step % GRID
        row = table[0, i]
        col = table[1, i]
        q = qz[j, i]
        do = doz[j, i]

        def window(stack, c):
            return stack[j, col + c, pl.ds(row, WINDOW)].reshape(WINDOW * TOK, HEAD)

        scores = [dot(window(kall, c), q, NT) * factor for c in range(WINDOW)]
        top = functools.reduce(jnp.maximum, [jnp.max(s, axis=0, keepdims=True) for s in scores])
        expo = [jnp.exp(s - top) for s in scores]
        total = sum(jnp.sum(e, axis=0, keepdims=True) for e in expo)
        inverse = 1.0 / total
        prob = [(e * inverse).astype(BF) for e in expo]
        att = sum(dot(window(vall, c), prob[c], TN) for c in range(WINDOW))
        delta = jnp.sum(att * do.astype(F32).T, axis=0, keepdims=True)
        o_out[i, j] = att.T.astype(BF)
        dq = jnp.zeros((HEAD, TOK), F32)
        for c in range(WINDOW):
            dprob = dot(window(vall, c), do, NT)
            dscore = (prob[c].astype(F32) * (dprob - delta) * factor).astype(BF)
            dq = dq + dot(window(kall, c), dscore, TN)
            spot = (j, col + c, pl.ds(row, WINDOW))
            dk[spot] += dot(dscore, q, NN).reshape(WINDOW, TOK, HEAD)
            dv[spot] += dot(prob[c], do, NN).reshape(WINDOW, TOK, HEAD)
        dq_out[i, j] = dq.T.astype(BF)
        return carry

    lax.fori_loop(0, GROUP * GRID, unit, 0)
    for j in range(GROUP):
        for c in range(GRID):
            for r in range(GRID):
                dk_out[c, r, j] = dk[j, c, r].astype(BF)
                dv_out[c, r, j] = dv[j, c, r].astype(BF)


RETURN_COPIES = 6 + 6 + 6 + 3 + 3 + 15 + 3 + 3


def return_kernel(
    o_ref, dq_ref, dk_ref, dv_ref, wt_ref, up_ref, downt_ref, og_ref, midg_ref,
    out, dq_out, dk_out, dv_out, grads,
    oh, dqh, dkh, dvh, rk, rv, ksum, vsum, att, ad, ry, zsrc, rz, dpsrc, rdp, full, send, recv,
):
    dp, sh, sw = place()
    sems = Sems(send, recv)
    row_peer = [(dp, turn(sh, d, GRID), sw) for d in (1, 2, 3)]
    col_peer = [(dp, sh, turn(sw, d, GRID)) for d in (1, 2, 3)]
    dp_peer = [(turn(dp, d, 16), sh, sw) for d in range(1, 16)]
    greet(row_peer + col_peer + dp_peer)

    k_in = [sems.copy(dk_ref.at[p[2]], rk.at[n], p) for n, p in enumerate(col_peer)]
    v_in = [sems.copy(dv_ref.at[p[2]], rv.at[n], p) for n, p in enumerate(col_peer)]
    home = pl.ds(sh * GROUP, GROUP)
    o_in = [sems.copy(o_ref.at[p[1]], oh.at[home], p) for p in row_peer]
    q_in = [sems.copy(dq_ref.at[p[1]], dqh.at[home], p) for p in row_peer]
    for j in range(GROUP):
        oh[sh * GROUP + j] = o_ref[sh, j]
        dqh[sh * GROUP + j] = dq_ref[sh, j]

    for made in o_in:
        made.wait_recv()
    for h in range(HEADS):
        att[:, h * HEAD : (h + 1) * HEAD] = oh[h]
    lora = dot(att[...], downt_ref[...], NT).astype(BF)
    ad[pl.ds(0, RANK), :] = dot(midg_ref[...], att[...], TN).astype(BF)
    ad[pl.ds(RANK, RANK), :] = dot(lora, og_ref[...], TN).astype(BF)

    part = 2 * RANK // GRID

    def strip(owner):
        return pl.ds(pl.multiple_of(owner * part, part), part)

    y_in = [sems.copy(ad.at[strip(p[2])], ry.at[n], p) for n, p in enumerate(col_peer)]
    for n in range(GRID):
        block = slice(n * SPAN, (n + 1) * SPAN)
        out[:, block] = (
            dot(att[...], wt_ref[block, :], NT) + dot(lora, up_ref[:, block], NN)
        ).astype(BF)

    for made in y_in:
        made.wait_recv()
    summed = ad[strip(sw), :].astype(F32)
    for n in range(3):
        summed = summed + ry[n].astype(F32)
    for n in range(GRID):
        zsrc[n] = summed[:, n * SPAN : (n + 1) * SPAN].astype(BF)
    z_in = [sems.copy(zsrc.at[p[1]], rz.at[n], p) for n, p in enumerate(row_peer)]

    back_in = []
    for made_in, own, got, total, there in (
        (k_in, dk_ref, rk, ksum, dkh),
        (v_in, dv_ref, rv, vsum, dvh),
    ):
        for made in made_in:
            made.wait_recv()
        for r in range(GRID):
            for j in range(GROUP):
                piece = own[sw, r, j].astype(F32)
                for n in range(3):
                    piece = piece + got[n, r, j].astype(F32)
                total[r, j] = piece.astype(BF)
        for p in row_peer:
            back_in.append(sems.copy(total.at[p[1]], there.at[home], p))
        for j in range(GROUP):
            there[sh * GROUP + j] = total[sh, j]

    for made in z_in:
        made.wait_recv()
    summed = zsrc[sh].astype(F32)
    for n in range(3):
        summed = summed + rz[n].astype(F32)
    dpsrc[...] = summed.astype(BF)
    rdp[dp] = dpsrc[...]
    d_in = [sems.copy(dpsrc, rdp.at[dp], p) for p in dp_peer]

    for made in q_in:
        made.wait_recv()
    for h in range(HEADS):
        dq_out[:, h * HEAD : (h + 1) * HEAD] = dqh[h]

    for made in d_in:
        made.wait_recv()
    summed = rdp[0].astype(F32)
    for n in range(1, 16):
        summed = summed + rdp[n].astype(F32)
    full[sw, sh] = summed.astype(BF)
    spot = full.at[sw, sh]
    g_in = [sems.copy(spot, spot, p) for p in row_peer]
    for made in g_in:
        made.wait_recv()
    spot = full.at[sw]
    h_in = [sems.copy(spot, spot, p) for p in col_peer]

    for made in back_in:
        made.wait_recv()
    for h in range(HEADS):
        dk_out[:, h * HEAD : (h + 1) * HEAD] = dkh[h]
        dv_out[:, h * HEAD : (h + 1) * HEAD] = dvh[h]
    for made in h_in:
        made.wait_recv()
    norm = TOKENS ** (-0.5)
    for c in range(GRID):
        for r in range(GRID):
            grads[c * part : (c + 1) * part, r * SPAN : (r + 1) * SPAN] = (
                full[c, r].astype(F32) * norm
            )
    for made in k_in + v_in + o_in + q_in + y_in + z_in + back_in + d_in + g_in + h_in:
        made.wait_send()


VM = pl.BlockSpec(memory_space=pltpu.VMEM)
SM = pl.BlockSpec(memory_space=pltpu.SMEM)
LIMIT = 48 << 20


def shaped(*dims, kind=BF):
    return jax.ShapeDtypeStruct(dims, kind)


def body(query, key, value, first_tile, weight, down, up, out_grad):
    shape = query.shape
    q, k, v, og = (a.reshape(TOK, FEAT) for a in (query, key, value, out_grad))
    wt_shard = weight.T
    downt = down.T
    stack = (GROUP, GRID, TOK, HEAD)
    grid = (GROUP, GRID, GRID, TOK, HEAD)
    heads = (HEADS, TOK, HEAD)
    dma = pltpu.SemaphoreType.DMA
    qz, kall, vall, doz, wt, midg = pl.pallas_call(
        spread_kernel,
        name="spread",
        out_shape=(
            shaped(*stack), shaped(*grid), shaped(*grid), shaped(*stack),
            shaped(FEAT, FEAT), shaped(TOK, RANK),
        ),
        in_specs=[VM] * 7,
        out_specs=[VM] * 6,
        scratch_shapes=[pltpu.VMEM(heads, BF)] * 4 + [dma((SPREAD_COPIES,)), dma((SPREAD_COPIES,))],
        compiler_params=pltpu.CompilerParams(
            collective_id=0, has_side_effects=True, vmem_limit_bytes=LIMIT
        ),
    )(q, k, v, og, wt_shard, downt, up)

    table = lax.dynamic_index_in_dim(first_tile, lax.axis_index("sw"), axis=2, keepdims=False)
    by_row = (GRID, GROUP, TOK, HEAD)
    by_spot = (GRID, GRID, GROUP, TOK, HEAD)
    o, dq, dk, dv = pl.pallas_call(
        attend_kernel,
        name="attend",
        out_shape=(shaped(*by_row), shaped(*by_row), shaped(*by_spot), shaped(*by_spot)),
        in_specs=[SM] + [VM] * 4,
        out_specs=[VM] * 4,
        scratch_shapes=[pltpu.VMEM(grid, F32)] * 2,
        compiler_params=pltpu.CompilerParams(vmem_limit_bytes=LIMIT),
    )(table, qz, doz, kall, vall)

    flat = (TOK, FEAT)
    part = 2 * RANK // GRID
    output, dq, dk, dv, grads = pl.pallas_call(
        return_kernel,
        name="bring_home",
        out_shape=(
            shaped(*flat), shaped(*flat), shaped(*flat), shaped(*flat),
            shaped(2 * RANK, FEAT, kind=F32),
        ),
        in_specs=[VM] * 9,
        out_specs=[VM] * 5,
        scratch_shapes=[
            pltpu.VMEM(heads, BF), pltpu.VMEM(heads, BF), pltpu.VMEM(heads, BF), pltpu.VMEM(heads, BF),
            pltpu.VMEM((3,) + by_row, BF), pltpu.VMEM((3,) + by_row, BF),
            pltpu.VMEM(by_row, BF), pltpu.VMEM(by_row, BF),
            pltpu.VMEM(flat, BF),
            pltpu.VMEM((2 * RANK, FEAT), BF),
            pltpu.VMEM((3, part, FEAT), BF),
            pltpu.VMEM((GRID, part, SPAN), BF),
            pltpu.VMEM((3, part, SPAN), BF),
            pltpu.VMEM((part, SPAN), BF),
            pltpu.VMEM((16, part, SPAN), BF),
            pltpu.VMEM((GRID, GRID, part, SPAN), BF),
            dma((RETURN_COPIES,)), dma((RETURN_COPIES,)),
        ],
        compiler_params=pltpu.CompilerParams(
            collective_id=1, has_side_effects=True, vmem_limit_bytes=LIMIT
        ),
    )(o, dq, dk, dv, wt, up, downt, og, midg)
    return (
        output.reshape(shape),
        dq.reshape(shape),
        dk.reshape(shape),
        dv.reshape(shape),
        grads[:RANK].T,
        grads[RANK:],
    )


def solution(mesh):
    tiles = P("dp", None, "sh", "sw", None)
    return jax.shard_map(
        body,
        mesh=mesh,
        in_specs=(tiles, tiles, tiles, P(), P(None, "dp"), P(), P(), tiles),
        out_specs=(tiles, tiles, tiles, tiles, P(), P()),
        check_vma=False,
    )
```

```python
import functools

import jax
import jax.numpy as jnp
from jax import lax
from jax.experimental import pallas as pl
from jax.experimental.pallas import tpu as pltpu
from jax.sharding import PartitionSpec as P

MESH = pl.DeviceIdType.MESH
HEADS = 12
HEAD = 128
WINDOW = 3
GROUP = 3
GRID = 4
TOK = 128
RANK = 64
FEAT = 1536
SPAN = GROUP * HEAD
SHARD = 96
TOKENS = 32768
BF = jnp.bfloat16
F32 = jnp.float32
NT = (((1,), (1,)), ((), ()))
TN = (((0,), (0,)), ((), ()))
NN = (((1,), (0,)), ((), ()))


def dot(a, b, dims):
    return lax.dot_general(a, b, dims, preferred_element_type=F32)


class Sems:
    def __init__(self, send, recv):
        self.send, self.recv, self.used = send, recv, 0

    def copy(self, src, dst, device):
        slot = self.used
        self.used += 1
        made = pltpu.make_async_remote_copy(
            src_ref=src,
            dst_ref=dst,
            send_sem=self.send.at[slot],
            recv_sem=self.recv.at[slot],
            device_id=device,
            device_id_type=MESH,
        )
        made.start()
        return made


def place():
    return lax.axis_index("dp"), lax.axis_index("sh"), lax.axis_index("sw")


def turn(index, by, size):
    return lax.rem(index + by, size)


def flip(dp, bit):
    return dp + bit - 2 * bit * lax.rem(lax.div(dp, bit), 2)


COPIES = 15 + 36 + 18 + 18 + 36 + 27


def kernel(
    table, q_hbm, k_hbm, v_hbm, og_hbm, w_hbm, down_hbm, up_hbm,
    out, dq_out, dk_out, dv_out, grads,
    q_in, k_in, v_in, og, w_in, downt, up,
    qs, ks, vs, dos, wt, mid,
    kj, vj, qj, doj, prob, att, dsl, oj, dqj, dkp, dvp,
    relk, relv, cmbk, cmbv, nearkv, farkv, sumk, sumv,
    oh, dqh, dkh, dvh, rows, ad, ry, zsrc, rz, dpsrc, rdp, full,
    local, send, recv,
):
    dp, sh, sw = place()
    sems = Sems(send, recv)
    factor = HEAD ** (-0.5)
    row_peer = [(dp, turn(sh, d, GRID), sw) for d in (1, 2, 3)]
    col_peer = [(dp, sh, turn(sw, d, GRID)) for d in (1, 2, 3)]
    dp_peer = [(turn(dp, d, 16), sh, sw) for d in range(1, 16)]
    after, before = col_peer[0], col_peer[2]
    east, west = dp_peer[3], dp_peer[11]
    mate = flip(dp, 2)
    zlo = (mate, sh, sw)
    twin = (flip(dp, 1), sh, sw)
    peers = row_peer + col_peer + dp_peer

    loads = []
    for n, (src, dst) in enumerate(
        ((w_hbm, w_in), (k_hbm, k_in), (v_hbm, v_in), (og_hbm, og), (up_hbm, up), (q_hbm, q_in), (down_hbm, downt))
    ):
        made = pltpu.make_async_copy(src, dst, local.at[n])
        made.start()
        loads.append(made)
    barrier = pltpu.get_barrier_semaphore()
    for device in peers:
        pl.semaphore_signal(barrier, inc=1, device_id=device, device_id_type=MESH)

    def shard_of(owner):
        return wt.at[pl.ds(pl.multiple_of(owner * SHARD, SHARD), SHARD)]

    def pass_on(owner, peer):
        return sems.copy(shard_of(owner), shard_of(owner), peer)

    loads[0].wait()
    wt[pl.ds(pl.multiple_of(dp * SHARD, SHARD), SHARD), :] = w_in[...]
    loads[1].wait()
    loads[2].wait()
    for h in range(HEADS):
        cols = slice(h * HEAD, (h + 1) * HEAD)
        ks[h] = k_in[:, cols]
        vs[h] = v_in[:, cols]
    pl.semaphore_wait(barrier, len(peers))

    done = []

    def scatter(stack, dst, j):
        made = [sems.copy(stack.at[p[1] * GROUP + j], dst, p) for p in row_peer]
        done.extend(made)
        return made

    def take(copies):
        for made in copies:
            made.wait_recv()

    def send_kv(j):
        return scatter(ks, kj[j].at[sw, sh], j) + scatter(vs, vj[j].at[sw, sh], j)

    kv = [send_kv(0)]
    mate_in = pass_on(dp, zlo)
    own_east, own_west = pass_on(dp, east), pass_on(dp, west)
    twin_in = [pass_on(dp, twin)]
    for j in range(GROUP):
        kj[j][sw, sh] = ks[sh * GROUP + j]
        vj[j][sw, sh] = vs[sh * GROUP + j]
    loads[3].wait()
    loads[4].wait()
    mid[...] = dot(og[...], up[...], NT).astype(BF)
    loads[5].wait()
    for h in range(HEADS):
        qs[h] = q_in[:, h * HEAD : (h + 1) * HEAD]
    for j in range(GROUP):
        qj[j][sh] = qs[sh * GROUP + j]
    loads[6].wait()

    mate_in.wait_recv()
    mate_east, mate_west = pass_on(mate, east), pass_on(mate, west)
    twin_in.append(pass_on(mate, twin))

    near, relay = [], []

    def spread_near(j):
        take(kv[j])
        near.append(
            (
                sems.copy(kj[j].at[sw], kj[j].at[sw], after),
                sems.copy(vj[j].at[sw], vj[j].at[sw], before),
                sems.copy(kj[j].at[sw], kj[j].at[sw], before),
                sems.copy(vj[j].at[sw], vj[j].at[sw], after),
            )
        )
        done.extend(near[j])

    def spread_far(j):
        take(near[j][:2])
        left, right = turn(sw, 3, GRID), turn(sw, 1, GRID)
        relay.append(
            (
                sems.copy(kj[j].at[left], kj[j].at[left], after),
                sems.copy(vj[j].at[right], vj[j].at[right], before),
            )
        )
        done.extend(relay[j])

    spread_near(0)
    kv.append(send_kv(1))
    q_got = [scatter(qs, qj[0].at[sh], 0)]

    def owner_at(step):
        return turn(dp, step, 16)

    own_east.wait_recv()
    own_far = pass_on(owner_at(12), east)
    twin_in.append(pass_on(owner_at(12), twin))
    own_west.wait_recv()
    twin_in.append(pass_on(owner_at(4), twin))

    spread_far(0)
    mate_west.wait_recv()
    mate_far = pass_on(flip(owner_at(4), 2), west)
    twin_in.append(pass_on(flip(owner_at(4), 2), twin))
    mate_east.wait_recv()
    twin_in.append(pass_on(flip(owner_at(12), 2), twin))

    spread_near(1)
    kv.append(send_kv(2))
    spread_far(1)
    own_far.wait_recv()
    twin_in.append(pass_on(owner_at(8), twin))
    mate_far.wait_recv()
    twin_in.append(pass_on(flip(owner_at(8), 2), twin))
    done.extend(twin_in + [mate_in, own_east, own_west, mate_east, mate_west, own_far, mate_far])
    spread_near(2)
    q_got.append(scatter(qs, qj[1].at[sh], 1))
    q_got.append(scatter(qs, qj[2].at[sh], 2))

    def window(stack, i, c):
        row, col = table[0, i, sw], table[1, i, sw]
        return stack[col + c, pl.ds(row, WINDOW)].reshape(WINDOW * TOK, HEAD)

    o_got = []

    def forward(j):
        take(near[j][2:])
        take(relay[j])
        take(q_got[j])

        def unit(i, carry):
            q = qj[j][i]
            scores = [dot(window(kj[j], i, c), q, NT) * factor for c in range(WINDOW)]
            top = functools.reduce(
                jnp.maximum, [jnp.max(s, axis=0, keepdims=True) for s in scores]
            )
            expo = [jnp.exp(s - top) for s in scores]
            total = sum(jnp.sum(e, axis=0, keepdims=True) for e in expo)
            inverse = 1.0 / total
            attended = jnp.zeros((HEAD, TOK), F32)
            for c in range(WINDOW):
                p = (expo[c] * inverse).astype(BF)
                prob[j, i, c] = p.reshape(WINDOW, TOK, TOK)
                attended = attended + dot(window(vj[j], i, c), p, TN)
            att[j, i] = attended
            oj[j][i] = attended.T.astype(BF)
            return carry

        lax.fori_loop(0, GRID, unit, 0)
        oh[sh * GROUP + j] = oj[j][sh]
        made = [sems.copy(oj[j].at[p[1]], oh.at[sh * GROUP + j], p) for p in row_peer]
        done.extend(made)
        o_got.extend(made)

    def project_back():
        take(twin_in)
        made = [[], [], []]
        for d in (1, 3, 2, 0):
            target = turn(sh, d, GRID)
            cols = pl.ds(pl.multiple_of(target * SPAN, HEAD), SPAN)
            part = dot(og[...], wt[:, cols], NN) + dot(mid[...], downt[:, cols], NN)
            part = part.astype(BF)
            for j in range(GROUP):
                piece = part[:, j * HEAD : (j + 1) * HEAD]
                if d:
                    dos[target * GROUP + j] = piece
                else:
                    doj[j][sh] = piece
        for j in range(GROUP):
            made[j] = scatter(dos, doj[j].at[sh], j)
        return made

    do_got = project_back()
    spread_far(2)
    forward(0)
    forward(1)
    forward(2)

    dq_got, rs_first, rs_second, back_got = [], [], [], []

    def backward(j):
        take(do_got[j])

        def unit(i, carry):
            do = doj[j][i]
            delta = jnp.sum(att[j, i] * do.astype(F32).T, axis=0, keepdims=True)
            dq = jnp.zeros((HEAD, TOK), F32)
            for c in range(WINDOW):
                dprob = dot(window(vj[j], i, c), do, NT)
                p = prob[j, i, c].reshape(WINDOW * TOK, TOK).astype(F32)
                dscore = (p * (dprob - delta) * factor).astype(BF)
                dsl[i, c] = dscore.reshape(WINDOW, TOK, TOK)
                dq = dq + dot(window(kj[j], i, c), dscore, TN)
            dqj[j][i] = dq.T.astype(BF)
            return carry

        lax.fori_loop(0, GRID, unit, 0)
        dqh[sh * GROUP + j] = dqj[j][sh]
        made = [sems.copy(dqj[j].at[p[1]], dqh.at[sh * GROUP + j], p) for p in row_peer]
        done.extend(made)
        dq_got.extend(made)
        q_all = qj[j][...].reshape(GRID * TOK, HEAD)
        do_all = doj[j][...].reshape(GRID * TOK, HEAD)

        def column(c, carry):
            def gathered(load):
                lines = []
                for r in range(GRID):
                    blocks = []
                    for i in range(GRID):
                        rr = r - table[0, i, sw]
                        cc = c - table[1, i, sw]
                        inside = (rr >= 0) & (rr < WINDOW) & (cc >= 0) & (cc < WINDOW)
                        block = load(i, jnp.clip(cc, 0, WINDOW - 1), jnp.clip(rr, 0, WINDOW - 1))
                        blocks.append(jnp.where(inside, block, jnp.zeros_like(block)))
                    lines.append(jnp.concatenate(blocks, axis=1))
                return jnp.concatenate(lines, axis=0)

            shape = (GRID, TOK, HEAD)
            dkp[j][c] = dot(gathered(lambda i, a, b: dsl[i, a, b]), q_all, NN).astype(BF).reshape(shape)
            dvp[j][c] = dot(gathered(lambda i, a, b: prob[j, i, a, b]), do_all, NN).astype(BF).reshape(shape)
            return carry

        lax.fori_loop(0, GRID, column, 0)
        one, two, three = (turn(sw, d, GRID) for d in (1, 2, 3))
        made = (
            sems.copy(dkp[j].at[two], relk.at[j], after),
            sems.copy(dvp[j].at[two], relv.at[j], before),
            sems.copy(dkp[j].at[three], nearkv.at[0, j], before),
            sems.copy(dvp[j].at[one], nearkv.at[1, j], after),
        )
        done.extend(made)
        rs_first.append(made)

    def combine(j):
        take(rs_first[j][:2])
        one, three = turn(sw, 1, GRID), turn(sw, 3, GRID)
        cmbk[j] = (relk[j].astype(F32) + dkp[j][one].astype(F32)).astype(BF)
        cmbv[j] = (relv[j].astype(F32) + dvp[j][three].astype(F32)).astype(BF)
        made = (
            sems.copy(cmbk.at[j], farkv.at[0, j], after),
            sems.copy(cmbv.at[j], farkv.at[1, j], before),
        )
        done.extend(made)
        rs_second.append(made)

    def finish(j):
        take(rs_first[j][2:])
        take(rs_second[j])
        for n, (own, total, there) in enumerate(((dkp, sumk, dkh), (dvp, sumv, dvh))):
            total[j] = (
                own[j][sw].astype(F32) + nearkv[n, j].astype(F32) + farkv[n, j].astype(F32)
            ).astype(BF)
            there[sh * GROUP + j] = total[j, sh]
            made = [sems.copy(total.at[j, p[1]], there.at[sh * GROUP + j], p) for p in row_peer]
            done.extend(made)
            back_got.extend(made)

    backward(0)
    backward(1)
    combine(0)
    backward(2)
    combine(1)

    take(o_got)
    for h in range(HEADS):
        rows[:, h * HEAD : (h + 1) * HEAD] = oh[h]
    lora = dot(rows[...], downt[...], NT).astype(BF)
    ad[pl.ds(0, RANK), :] = dot(mid[...], rows[...], TN).astype(BF)
    ad[pl.ds(RANK, RANK), :] = dot(lora, og[...], TN).astype(BF)
    part = 2 * RANK // GRID

    def strip(owner):
        return pl.ds(pl.multiple_of(owner * part, part), part)

    y_got = [sems.copy(ad.at[strip(p[2])], ry.at[n], p) for n, p in enumerate(col_peer)]
    finish(0)
    combine(2)
    for n in range(GRID):
        block = slice(n * SPAN, (n + 1) * SPAN)
        out[:, block] = (
            dot(rows[...], wt[block, :], NT) + dot(lora, up[:, block], NN)
        ).astype(BF)

    take(y_got)
    summed = ad[strip(sw), :].astype(F32)
    for n in range(3):
        summed = summed + ry[n].astype(F32)
    for n in range(GRID):
        zsrc[n] = summed[:, n * SPAN : (n + 1) * SPAN].astype(BF)
    z_got = [sems.copy(zsrc.at[p[1]], rz.at[n], p) for n, p in enumerate(row_peer)]
    finish(1)

    take(z_got)
    summed = zsrc[sh].astype(F32)
    for n in range(3):
        summed = summed + rz[n].astype(F32)
    dpsrc[...] = summed.astype(BF)
    rdp[dp] = dpsrc[...]
    d_got = [sems.copy(dpsrc, rdp.at[dp], p) for p in dp_peer]
    finish(2)

    take(dq_got)
    for h in range(HEADS):
        dq_out[:, h * HEAD : (h + 1) * HEAD] = dqh[h]

    take(d_got)
    summed = rdp[0].astype(F32)
    for n in range(1, 16):
        summed = summed + rdp[n].astype(F32)
    full[sw, sh] = summed.astype(BF)
    spot = full.at[sw, sh]
    g_got = [sems.copy(spot, spot, p) for p in row_peer]
    take(g_got)
    spot = full.at[sw]
    h_got = [sems.copy(spot, spot, p) for p in col_peer]

    take(back_got)
    for h in range(HEADS):
        dk_out[:, h * HEAD : (h + 1) * HEAD] = dkh[h]
        dv_out[:, h * HEAD : (h + 1) * HEAD] = dvh[h]
    take(h_got)
    norm = TOKENS ** (-0.5)
    for c in range(GRID):
        for r in range(GRID):
            grads[c * part : (c + 1) * part, r * SPAN : (r + 1) * SPAN] = (
                full[c, r].astype(F32) * norm
            )
    for made in done + y_got + z_got + d_got + g_got + h_got:
        made.wait_send()


VM = pl.BlockSpec(memory_space=pltpu.VMEM)
SM = pl.BlockSpec(memory_space=pltpu.SMEM)
ANY = pl.BlockSpec(memory_space=pl.ANY)


def shaped(*dims, kind=BF):
    return jax.ShapeDtypeStruct(dims, kind)


def body(query, key, value, first_tile, weight, down, up, out_grad):
    shape = query.shape
    q, k, v, og = (a.reshape(TOK, FEAT) for a in (query, key, value, out_grad))
    dma = pltpu.SemaphoreType.DMA
    flat = (TOK, FEAT)
    part = 2 * RANK // GRID
    tiles = (GRID, TOK, HEAD)

    def buf(*dims, kind=BF):
        return pltpu.VMEM(dims, kind)

    def each(*dims):
        return [buf(*dims) for _ in range(GROUP)]

    output, dq, dk, dv, grads = pl.pallas_call(
        kernel,
        name="attend",
        out_shape=(
            shaped(*flat), shaped(*flat), shaped(*flat), shaped(*flat),
            shaped(2 * RANK, FEAT, kind=F32),
        ),
        in_specs=[SM] + [ANY] * 7,
        out_specs=[VM] * 5,
        scratch_shapes=[
            buf(*flat), buf(*flat), buf(*flat), buf(*flat), buf(SHARD, FEAT), buf(RANK, FEAT), buf(RANK, FEAT),
            buf(HEADS, TOK, HEAD), buf(HEADS, TOK, HEAD), buf(HEADS, TOK, HEAD), buf(HEADS, TOK, HEAD),
            buf(FEAT, FEAT), buf(TOK, RANK),
            each(GRID, *tiles), each(GRID, *tiles), each(*tiles), each(*tiles),
            buf(GROUP, GRID, WINDOW, WINDOW, TOK, TOK), buf(GROUP, GRID, HEAD, TOK, kind=F32),
            buf(GRID, WINDOW, WINDOW, TOK, TOK), each(*tiles), each(*tiles),
            each(GRID, *tiles), each(GRID, *tiles),
            buf(GROUP, *tiles), buf(GROUP, *tiles), buf(GROUP, *tiles), buf(GROUP, *tiles),
            buf(2, GROUP, *tiles), buf(2, GROUP, *tiles), buf(GROUP, *tiles), buf(GROUP, *tiles),
            buf(HEADS, TOK, HEAD), buf(HEADS, TOK, HEAD), buf(HEADS, TOK, HEAD), buf(HEADS, TOK, HEAD),
            buf(*flat), buf(2 * RANK, FEAT), buf(3, part, FEAT), buf(GRID, part, SPAN),
            buf(3, part, SPAN), buf(part, SPAN), buf(16, part, SPAN), buf(GRID, GRID, part, SPAN),
            dma((7,)), dma((COPIES,)), dma((COPIES,)),
        ],
        compiler_params=pltpu.CompilerParams(
            collective_id=0, has_side_effects=True, vmem_limit_bytes=56 << 20
        ),
    )(first_tile, q, k, v, og, weight.T, down.T, up)
    return (
        output.reshape(shape),
        dq.reshape(shape),
        dk.reshape(shape),
        dv.reshape(shape),
        grads[:RANK].T,
        grads[RANK:],
    )


def solution(mesh):
    tiles = P("dp", None, "sh", "sw", None)
    return jax.shard_map(
        body,
        mesh=mesh,
        in_specs=(tiles, tiles, tiles, P(), P(None, "dp"), P(), P(), tiles),
        out_specs=(tiles, tiles, tiles, tiles, P(), P()),
        check_vma=False,
    )
```

```python
import functools

import jax
import jax.numpy as jnp
from jax import lax
from jax.experimental import pallas as pl
from jax.experimental.pallas import tpu as pltpu
from jax.sharding import PartitionSpec as P

MESH = pl.DeviceIdType.MESH
HEADS = 12
HEAD = 128
WINDOW = 3
GROUP = 3
GRID = 4
TOK = 128
RANK = 64
FEAT = 1536
SPAN = GROUP * HEAD
SHARD = 96
TOKENS = 32768
BF = jnp.bfloat16
F32 = jnp.float32
NT = (((1,), (1,)), ((), ()))
TN = (((0,), (0,)), ((), ()))
NN = (((1,), (0,)), ((), ()))


def dot(a, b, dims):
    return lax.dot_general(a, b, dims, preferred_element_type=F32)


class Sems:
    def __init__(self, send, recv):
        self.send, self.recv, self.used = send, recv, 0

    def copy(self, src, dst, device):
        slot = self.used
        self.used += 1
        made = pltpu.make_async_remote_copy(
            src_ref=src,
            dst_ref=dst,
            send_sem=self.send.at[slot],
            recv_sem=self.recv.at[slot],
            device_id=device,
            device_id_type=MESH,
        )
        made.start()
        return made


def place():
    return lax.axis_index("dp"), lax.axis_index("sh"), lax.axis_index("sw")


def turn(index, by, size):
    return lax.rem(index + by, size)


def flip(dp, bit):
    return dp + bit - 2 * bit * lax.rem(lax.div(dp, bit), 2)


COPIES = 16 + 36 + 18 + 18 + 36 + 27


def kernel(
    table, q_hbm, k_hbm, v_hbm, og_hbm, w_hbm, down_hbm, up_hbm,
    out_hbm, dq_hbm, dk_hbm, dv_hbm, down_grad_hbm, up_grad_hbm,
    out, dq_out, dk_out, dv_out, down_grad, up_grad,
    q_in, k_in, v_in, og, w_in, downt, up,
    qs, ks, vs, dos, wt, mid,
    kj, vj, qj, doj, prob, att, dsl, oj, dqj, dkp, dvp,
    relk, relv, cmbk, cmbv, nearkv, farkv, sumk, sumv,
    oh, dqh, dkh, dvh, rows, ad, ry, zsrc, rz, dpsrc, rdp, full,
    local, storing, send, recv,
):
    dp, sh, sw = place()
    sems = Sems(send, recv)
    factor = HEAD ** (-0.5)
    row_peer = [(dp, turn(sh, d, GRID), sw) for d in (1, 2, 3)]
    col_peer = [(dp, sh, turn(sw, d, GRID)) for d in (1, 2, 3)]
    dp_peer = [(turn(dp, d, 16), sh, sw) for d in range(1, 16)]
    after, before = col_peer[0], col_peer[2]
    east, west = dp_peer[3], dp_peer[11]
    mate = flip(dp, 2)
    zlo = (mate, sh, sw)
    low = lax.rem(lax.div(dp, 2), 2)
    zlo_over = (mate, turn(sh, 3 + 2 * low, GRID), sw)
    twin = (flip(dp, 1), sh, sw)
    peers = row_peer + col_peer + dp_peer + [zlo_over]

    loads = []
    for n, (src, dst) in enumerate(
        ((w_hbm, w_in), (k_hbm, k_in), (v_hbm, v_in), (og_hbm, og), (up_hbm, up), (q_hbm, q_in), (down_hbm, downt))
    ):
        made = pltpu.make_async_copy(src, dst, local.at[n])
        made.start()
        loads.append(made)
    barrier = pltpu.get_barrier_semaphore()
    for device in peers:
        pl.semaphore_signal(barrier, inc=1, device_id=device, device_id_type=MESH)

    def shard_of(owner):
        return wt.at[pl.ds(pl.multiple_of(owner * SHARD, SHARD), SHARD)]

    def half_of(owner, n):
        start = pl.multiple_of(owner * SHARD + n * (SHARD // 2), SHARD // 2)
        return wt.at[pl.ds(start, SHARD // 2)]

    def pass_on(owner, peer):
        return sems.copy(shard_of(owner), shard_of(owner), peer)

    loads[0].wait()
    wt[pl.ds(pl.multiple_of(dp * SHARD, SHARD), SHARD), :] = w_in[...]
    loads[1].wait()
    loads[2].wait()
    for h in range(HEADS):
        cols = slice(h * HEAD, (h + 1) * HEAD)
        ks[h] = k_in[:, cols]
        vs[h] = v_in[:, cols]
    pl.semaphore_wait(barrier, len(peers))

    done = []

    def scatter(stack, dst, j):
        made = [sems.copy(stack.at[p[1] * GROUP + j], dst, p) for p in row_peer]
        done.extend(made)
        return made

    def take(copies):
        for made in copies:
            made.wait_recv()

    def send_kv(j):
        return scatter(ks, kj[j].at[sw, sh], j) + scatter(vs, vj[j].at[sw, sh], j)

    kv = [send_kv(0)]
    mate_in = [
        sems.copy(half_of(dp, n), half_of(dp, n), peer) for n, peer in enumerate((zlo, zlo_over))
    ]
    own_east, own_west = pass_on(dp, east), pass_on(dp, west)
    twin_in = [pass_on(dp, twin)]
    for j in range(GROUP):
        kj[j][sw, sh] = ks[sh * GROUP + j]
        vj[j][sw, sh] = vs[sh * GROUP + j]
    loads[3].wait()
    loads[4].wait()
    mid[...] = dot(og[...], up[...], NT).astype(BF)
    loads[5].wait()
    for h in range(HEADS):
        qs[h] = q_in[:, h * HEAD : (h + 1) * HEAD]
    for j in range(GROUP):
        qj[j][sh] = qs[sh * GROUP + j]
    loads[6].wait()

    near, relay = [], []

    def spread_near(j):
        take(kv[j])
        near.append(
            (
                sems.copy(kj[j].at[sw], kj[j].at[sw], after),
                sems.copy(vj[j].at[sw], vj[j].at[sw], before),
                sems.copy(kj[j].at[sw], kj[j].at[sw], before),
                sems.copy(vj[j].at[sw], vj[j].at[sw], after),
            )
        )
        done.extend(near[j])

    def spread_far(j):
        take(near[j][:2])
        left, right = turn(sw, 3, GRID), turn(sw, 1, GRID)
        relay.append(
            (
                sems.copy(kj[j].at[left], kj[j].at[left], after),
                sems.copy(vj[j].at[right], vj[j].at[right], before),
            )
        )
        done.extend(relay[j])

    def owner_at(step):
        return turn(dp, step, 16)

    kv.append(send_kv(1))
    take(mate_in)
    mate_east, mate_west = pass_on(mate, east), pass_on(mate, west)
    twin_in.append(pass_on(mate, twin))
    spread_near(0)
    q_got = [scatter(qs, qj[0].at[sh], 0)]
    kv.append(send_kv(2))
    own_east.wait_recv()
    own_far = pass_on(owner_at(12), east)
    twin_in.append(pass_on(owner_at(12), twin))
    own_west.wait_recv()
    twin_in.append(pass_on(owner_at(4), twin))
    spread_far(0)
    spread_near(1)
    q_got.append(scatter(qs, qj[1].at[sh], 1))
    q_got.append(scatter(qs, qj[2].at[sh], 2))
    mate_west.wait_recv()
    mate_far = pass_on(flip(owner_at(4), 2), west)
    twin_in.append(pass_on(flip(owner_at(4), 2), twin))
    mate_east.wait_recv()
    twin_in.append(pass_on(flip(owner_at(12), 2), twin))
    own_far.wait_recv()
    twin_in.append(pass_on(owner_at(8), twin))
    mate_far.wait_recv()
    twin_in.append(pass_on(flip(owner_at(8), 2), twin))
    spread_far(1)
    spread_near(2)
    done.extend(twin_in + mate_in + [own_east, own_west, mate_east, mate_west, own_far, mate_far])

    def window(stack, i, c):
        row, col = table[0, i, sw], table[1, i, sw]
        return stack[col + c, pl.ds(row, WINDOW)].reshape(WINDOW * TOK, HEAD)

    o_got = []

    def forward(j):
        take(near[j][2:])
        take(relay[j])
        take(q_got[j])

        def unit(i, carry):
            q = qj[j][i]
            scores = [dot(window(kj[j], i, c), q, NT) * factor for c in range(WINDOW)]
            top = functools.reduce(
                jnp.maximum, [jnp.max(s, axis=0, keepdims=True) for s in scores]
            )
            expo = [jnp.exp(s - top) for s in scores]
            total = sum(jnp.sum(e, axis=0, keepdims=True) for e in expo)
            inverse = 1.0 / total
            attended = jnp.zeros((HEAD, TOK), F32)
            for c in range(WINDOW):
                p = (expo[c] * inverse).astype(BF)
                prob[j, i, c] = p.reshape(WINDOW, TOK, TOK)
                attended = attended + dot(window(vj[j], i, c), p, TN)
            att[j, i] = attended
            oj[j][i] = attended.T.astype(BF)
            return carry

        lax.fori_loop(0, GRID, unit, 0)
        oh[sh * GROUP + j] = oj[j][sh]
        made = [sems.copy(oj[j].at[p[1]], oh.at[sh * GROUP + j], p) for p in row_peer]
        done.extend(made)
        o_got.extend(made)

    def project_back():
        take(twin_in)
        made = [[], [], []]
        for d in (1, 3, 2, 0):
            target = turn(sh, d, GRID)
            cols = pl.ds(pl.multiple_of(target * SPAN, HEAD), SPAN)
            part = dot(og[...], wt[:, cols], NN) + dot(mid[...], downt[:, cols], NN)
            part = part.astype(BF)
            for j in range(GROUP):
                piece = part[:, j * HEAD : (j + 1) * HEAD]
                if d:
                    dos[target * GROUP + j] = piece
                else:
                    doj[j][sh] = piece
            if d:
                peer = (dp, target, sw)
                made[0].append(sems.copy(dos.at[target * GROUP], doj[0].at[sh], peer))
        done.extend(made[0])
        return made

    dq_got, rs_first, rs_second, back_got = [], [], [], []

    def backward(j):
        take(do_got[j])

        def unit(i, carry):
            do = doj[j][i]
            delta = jnp.sum(att[j, i] * do.astype(F32).T, axis=0, keepdims=True)
            dq = jnp.zeros((HEAD, TOK), F32)
            for c in range(WINDOW):
                dprob = dot(window(vj[j], i, c), do, NT)
                p = prob[j, i, c].reshape(WINDOW * TOK, TOK).astype(F32)
                dscore = (p * (dprob - delta) * factor).astype(BF)
                dsl[i, c] = dscore.reshape(WINDOW, TOK, TOK)
                dq = dq + dot(window(kj[j], i, c), dscore, TN)
            dqj[j][i] = dq.T.astype(BF)
            return carry

        q_all = qj[j][...].reshape(GRID * TOK, HEAD)
        do_all = doj[j][...].reshape(GRID * TOK, HEAD)
        one, two, three = (turn(sw, d, GRID) for d in (1, 2, 3))

        def sum_columns(load, other, total):
            def column(c, carry):
                lines = []
                for r in range(GRID):
                    blocks = []
                    for i in range(GRID):
                        rr = r - table[0, i, sw]
                        cc = c - table[1, i, sw]
                        inside = (rr >= 0) & (rr < WINDOW) & (cc >= 0) & (cc < WINDOW)
                        block = load(i, jnp.clip(cc, 0, WINDOW - 1), jnp.clip(rr, 0, WINDOW - 1))
                        blocks.append(jnp.where(inside, block, jnp.zeros_like(block)))
                    lines.append(jnp.concatenate(blocks, axis=1))
                lines = jnp.concatenate(lines, axis=0)
                total[c] = dot(lines, other, NN).astype(BF).reshape(GRID, TOK, HEAD)
                return carry

            lax.fori_loop(0, GRID, column, 0)

        sum_columns(lambda i, a, b: prob[j, i, a, b], do_all, dvp[j])
        v_far = sems.copy(dvp[j].at[two], relv.at[j], before)
        v_near = sems.copy(dvp[j].at[one], nearkv.at[1, j], after)
        lax.fori_loop(0, GRID, unit, 0)
        sum_columns(lambda i, a, b: dsl[i, a, b], q_all, dkp[j])
        k_far = sems.copy(dkp[j].at[two], relk.at[j], after)
        k_near = sems.copy(dkp[j].at[three], nearkv.at[0, j], before)
        rs_first.append((k_far, v_far, k_near, v_near))
        done.extend(rs_first[j])
        dqh[sh * GROUP + j] = dqj[j][sh]
        made = [sems.copy(dqj[j].at[p[1]], dqh.at[sh * GROUP + j], p) for p in row_peer]
        done.extend(made)
        dq_got.extend(made)

    def combine(j):
        take(rs_first[j][:2])
        one, three = turn(sw, 1, GRID), turn(sw, 3, GRID)
        cmbk[j] = (relk[j].astype(F32) + dkp[j][one].astype(F32)).astype(BF)
        cmbv[j] = (relv[j].astype(F32) + dvp[j][three].astype(F32)).astype(BF)
        made = (
            sems.copy(cmbk.at[j], farkv.at[0, j], after),
            sems.copy(cmbv.at[j], farkv.at[1, j], before),
        )
        done.extend(made)
        rs_second.append(made)

    def finish(j):
        take(rs_first[j][2:])
        take(rs_second[j])
        for n, (own, total, there) in enumerate(((dkp, sumk, dkh), (dvp, sumv, dvh))):
            total[j] = (
                own[j][sw].astype(F32) + nearkv[n, j].astype(F32) + farkv[n, j].astype(F32)
            ).astype(BF)
            there[sh * GROUP + j] = total[j, sh]
            made = [sems.copy(total.at[j, p[1]], there.at[sh * GROUP + j], p) for p in row_peer]
            done.extend(made)
            back_got.extend(made)

    part = 2 * RANK // GRID

    def strip(owner):
        return pl.ds(pl.multiple_of(owner * part, part), part)

    def write_out(n, src, dst):
        made = pltpu.make_async_copy(src, dst, storing.at[n])
        made.start()
        return made

    def project(blocks):
        for n in blocks:
            block = slice(n * SPAN, (n + 1) * SPAN)
            out[:, block] = (
                dot(rows[...], wt[block, :], NT) + dot(lora, up[:, block], NN)
            ).astype(BF)

    forward(0)
    do_got = project_back()
    forward(1)
    spread_far(2)
    do_got[1] = scatter(dos, doj[1].at[sh], 1)
    backward(0)
    do_got[2] = scatter(dos, doj[2].at[sh], 2)
    forward(2)
    backward(1)
    combine(0)

    take(o_got)
    for h in range(HEADS):
        rows[:, h * HEAD : (h + 1) * HEAD] = oh[h]
    lora = dot(rows[...], downt[...], NT).astype(BF)
    ad[pl.ds(0, RANK), :] = dot(mid[...], rows[...], TN).astype(BF)
    ad[pl.ds(RANK, RANK), :] = dot(lora, og[...], TN).astype(BF)
    y_got = [sems.copy(ad.at[strip(p[2])], ry.at[n], p) for n, p in enumerate(col_peer)]
    backward(2)
    combine(1)

    take(y_got)
    summed = ad[strip(sw), :].astype(F32)
    for n in range(3):
        summed = summed + ry[n].astype(F32)
    for n in range(GRID):
        zsrc[n] = summed[:, n * SPAN : (n + 1) * SPAN].astype(BF)
    z_got = [sems.copy(zsrc.at[p[1]], rz.at[n], p) for n, p in enumerate(row_peer)]
    finish(0)
    project((0, 1))

    take(z_got)
    summed = zsrc[sh].astype(F32)
    for n in range(3):
        summed = summed + rz[n].astype(F32)
    dpsrc[...] = summed.astype(BF)
    rdp[dp] = dpsrc[...]
    d_got = [sems.copy(dpsrc, rdp.at[dp], p) for p in dp_peer]
    combine(2)
    finish(1)
    project((2, 3))
    stores = [write_out(0, out, out_hbm)]

    take(d_got)
    summed = rdp[0].astype(F32)
    for n in range(1, 16):
        summed = summed + rdp[n].astype(F32)
    full[sw, sh] = summed.astype(BF)
    spot = full.at[sw, sh]
    g_got = [sems.copy(spot, spot, p) for p in row_peer]
    finish(2)

    take(g_got)
    spot = full.at[sw]
    h_got = [sems.copy(spot, spot, p) for p in col_peer]
    take(dq_got)
    for h in range(HEADS):
        dq_out[:, h * HEAD : (h + 1) * HEAD] = dqh[h]
    stores.append(write_out(1, dq_out, dq_hbm))

    take(h_got)
    norm = TOKENS ** (-0.5)
    for c in range(GRID):
        half = down_grad if c < GRID // 2 else up_grad
        start = (c % (GRID // 2)) * part
        for r in range(GRID):
            half[start : start + part, r * SPAN : (r + 1) * SPAN] = full[c, r].astype(F32) * norm
    stores.append(write_out(2, down_grad, down_grad_hbm))
    stores.append(write_out(3, up_grad, up_grad_hbm))

    take(back_got)
    for h in range(HEADS):
        dk_out[:, h * HEAD : (h + 1) * HEAD] = dkh[h]
        dv_out[:, h * HEAD : (h + 1) * HEAD] = dvh[h]
    stores.append(write_out(4, dk_out, dk_hbm))
    stores.append(write_out(5, dv_out, dv_hbm))
    for made in done + y_got + z_got + d_got + g_got + h_got:
        made.wait_send()
    for made in stores:
        made.wait()


def finish_kernel(*refs):
    count = len(refs) // 3
    sems = refs[-1]
    here = refs[2 * count : 3 * count]
    reads = [pltpu.make_async_copy(refs[n], here[n], sems.at[0, n]) for n in range(count)]
    writes = [pltpu.make_async_copy(here[n], refs[count + n], sems.at[1, n]) for n in range(count)]
    for copy in reads:
        copy.start()
    for n in range(count):
        reads[n].wait()
        writes[n].start()
    for copy in writes:
        copy.wait()


SM = pl.BlockSpec(memory_space=pltpu.SMEM)
ANY = pl.BlockSpec(memory_space=pl.ANY)


def shaped(*dims, kind=BF):
    return jax.ShapeDtypeStruct(dims, kind)


def body(query, key, value, first_tile, weight, down, up, out_grad):
    shape = query.shape
    q, k, v, og = (a.reshape(TOK, FEAT) for a in (query, key, value, out_grad))
    dma = pltpu.SemaphoreType.DMA
    flat = (TOK, FEAT)
    part = 2 * RANK // GRID
    tiles = (GRID, TOK, HEAD)

    def buf(*dims, kind=BF):
        return pltpu.VMEM(dims, kind)

    def each(*dims):
        return [buf(*dims) for _ in range(GROUP)]

    results = (
        shaped(*flat), shaped(*flat), shaped(*flat), shaped(*flat),
        shaped(RANK, FEAT, kind=F32), shaped(RANK, FEAT, kind=F32),
    )
    made = pl.pallas_call(
        kernel,
        name="attend",
        out_shape=results,
        in_specs=[SM] + [ANY] * 7,
        out_specs=[ANY] * 6,
        scratch_shapes=[
            buf(*flat), buf(*flat), buf(*flat), buf(*flat), buf(RANK, FEAT, kind=F32), buf(RANK, FEAT, kind=F32),
            buf(*flat), buf(*flat), buf(*flat), buf(*flat), buf(SHARD, FEAT), buf(RANK, FEAT), buf(RANK, FEAT),
            buf(HEADS, TOK, HEAD), buf(HEADS, TOK, HEAD), buf(HEADS, TOK, HEAD), buf(HEADS, TOK, HEAD),
            buf(FEAT, FEAT), buf(TOK, RANK),
            each(GRID, *tiles), each(GRID, *tiles), each(*tiles), each(*tiles),
            buf(GROUP, GRID, WINDOW, WINDOW, TOK, TOK), buf(GROUP, GRID, HEAD, TOK, kind=F32),
            buf(GRID, WINDOW, WINDOW, TOK, TOK), each(*tiles), each(*tiles),
            each(GRID, *tiles), each(GRID, *tiles),
            buf(GROUP, *tiles), buf(GROUP, *tiles), buf(GROUP, *tiles), buf(GROUP, *tiles),
            buf(2, GROUP, *tiles), buf(2, GROUP, *tiles), buf(GROUP, *tiles), buf(GROUP, *tiles),
            buf(HEADS, TOK, HEAD), buf(HEADS, TOK, HEAD), buf(HEADS, TOK, HEAD), buf(HEADS, TOK, HEAD),
            buf(*flat), buf(2 * RANK, FEAT), buf(3, part, FEAT), buf(GRID, part, SPAN),
            buf(3, part, SPAN), buf(part, SPAN), buf(16, part, SPAN), buf(GRID, GRID, part, SPAN),
            dma((7,)), dma((6,)), dma((COPIES,)), dma((COPIES,)),
        ],
        compiler_params=pltpu.CompilerParams(
            collective_id=0, has_side_effects=True, vmem_limit_bytes=56 << 20
        ),
    )(first_tile, q, k, v, og, weight.T, down.T, up)
    output, dq, dk, dv, down_grad, up_grad = pl.pallas_call(
        finish_kernel,
        name="finish",
        out_shape=results,
        in_specs=[ANY] * 6,
        out_specs=[ANY] * 6,
        scratch_shapes=[pltpu.VMEM(r.shape, r.dtype) for r in results] + [dma((2, 6))],
    )(*made)
    return (
        output.reshape(shape),
        dq.reshape(shape),
        dk.reshape(shape),
        dv.reshape(shape),
        down_grad.T,
        up_grad,
    )


def solution(mesh):
    tiles = P("dp", None, "sh", "sw", None)
    return jax.shard_map(
        body,
        mesh=mesh,
        in_specs=(tiles, tiles, tiles, P(), P(None, "dp"), P(), P(), tiles),
        out_specs=(tiles, tiles, tiles, tiles, P(), P()),
        check_vma=False,
    )
```

```python
import functools

import jax
import jax.numpy as jnp
from jax import lax
from jax.experimental import pallas as pl
from jax.experimental.pallas import tpu as pltpu
from jax.sharding import PartitionSpec as P

MESH = pl.DeviceIdType.MESH
HEADS = 12
HEAD = 128
WINDOW = 3
GROUP = 3
GRID = 4
TOK = 128
RANK = 64
FEAT = 1536
SPAN = GROUP * HEAD
SHARD = 96
TOKENS = 32768
BF = jnp.bfloat16
F32 = jnp.float32
NT = (((1,), (1,)), ((), ()))
TN = (((0,), (0,)), ((), ()))
NN = (((1,), (0,)), ((), ()))


def dot(a, b, dims):
    return lax.dot_general(a, b, dims, preferred_element_type=F32)


class Sems:
    def __init__(self, send, recv):
        self.send, self.recv, self.used = send, recv, 0

    def copy(self, src, dst, device):
        slot = self.used
        self.used += 1
        made = pltpu.make_async_remote_copy(
            src_ref=src,
            dst_ref=dst,
            send_sem=self.send.at[slot],
            recv_sem=self.recv.at[slot],
            device_id=device,
            device_id_type=MESH,
        )
        made.start()
        return made


def place():
    return lax.axis_index("dp"), lax.axis_index("sh"), lax.axis_index("sw")


def turn(index, by, size):
    return lax.rem(index + by, size)


def flip(dp, bit):
    return dp + bit - 2 * bit * lax.rem(lax.div(dp, bit), 2)


COPIES = 16 + 36 + 18 + 18 + 36 + 27


def kernel(
    table, q_hbm, k_hbm, v_hbm, og_hbm, w_hbm, down_hbm, up_hbm,
    out, dq_out, dk_out, dv_out, down_grad, up_grad,
    q_in, k_in, v_in, og, w_in, downt, up,
    qs, ks, vs, dos, wt, mid,
    kj, vj, qj, doj, prob, att, dsl, oj, dqj, dkp, dvp,
    relk, relv, cmbk, cmbv, nearkv, farkv, sumk, sumv,
    oh, dqh, dkh, dvh, rows, ad, ry, zsrc, rz, dpsrc, rdp, full,
    local, send, recv,
):
    dp, sh, sw = place()
    sems = Sems(send, recv)
    factor = HEAD ** (-0.5)
    row_peer = [(dp, turn(sh, d, GRID), sw) for d in (1, 2, 3)]
    col_peer = [(dp, sh, turn(sw, d, GRID)) for d in (1, 2, 3)]
    dp_peer = [(turn(dp, d, 16), sh, sw) for d in range(1, 16)]
    after, before = col_peer[0], col_peer[2]
    east, west = dp_peer[3], dp_peer[11]
    mate = flip(dp, 2)
    zlo = (mate, sh, sw)
    low = lax.rem(lax.div(dp, 2), 2)
    zlo_over = (mate, turn(sh, 3 + 2 * low, GRID), sw)
    twin = (flip(dp, 1), sh, sw)
    peers = row_peer + col_peer + dp_peer + [zlo_over]

    loads = []
    for n, (src, dst) in enumerate(
        ((w_hbm, w_in), (k_hbm, k_in), (v_hbm, v_in), (og_hbm, og), (up_hbm, up), (q_hbm, q_in), (down_hbm, downt))
    ):
        made = pltpu.make_async_copy(src, dst, local.at[n])
        made.start()
        loads.append(made)
    barrier = pltpu.get_barrier_semaphore()
    for device in peers:
        pl.semaphore_signal(barrier, inc=1, device_id=device, device_id_type=MESH)

    def shard_of(owner):
        return wt.at[pl.ds(pl.multiple_of(owner * SHARD, SHARD), SHARD)]

    def half_of(owner, n):
        start = pl.multiple_of(owner * SHARD + n * (SHARD // 2), SHARD // 2)
        return wt.at[pl.ds(start, SHARD // 2)]

    def pass_on(owner, peer):
        return sems.copy(shard_of(owner), shard_of(owner), peer)

    loads[0].wait()
    wt[pl.ds(pl.multiple_of(dp * SHARD, SHARD), SHARD), :] = w_in[...]
    loads[1].wait()
    loads[2].wait()
    for h in range(HEADS):
        cols = slice(h * HEAD, (h + 1) * HEAD)
        ks[h] = k_in[:, cols]
        vs[h] = v_in[:, cols]
    pl.semaphore_wait(barrier, len(peers))

    done = []

    def scatter(stack, dst, j):
        made = [sems.copy(stack.at[p[1] * GROUP + j], dst, p) for p in row_peer]
        done.extend(made)
        return made

    def settle():
        while done:
            done.pop().wait_send()

    def take(copies):
        for made in copies:
            made.wait_recv()

    def send_kv(j):
        return scatter(ks, kj[j].at[sw, sh], j) + scatter(vs, vj[j].at[sw, sh], j)

    kv = [send_kv(0)]
    mate_in = [
        sems.copy(half_of(dp, n), half_of(dp, n), peer) for n, peer in enumerate((zlo, zlo_over))
    ]
    own_east, own_west = pass_on(dp, east), pass_on(dp, west)
    twin_in = [pass_on(dp, twin)]
    for j in range(GROUP):
        kj[j][sw, sh] = ks[sh * GROUP + j]
        vj[j][sw, sh] = vs[sh * GROUP + j]
    loads[3].wait()
    loads[4].wait()
    mid[...] = dot(og[...], up[...], NT).astype(BF)
    loads[5].wait()
    for h in range(HEADS):
        qs[h] = q_in[:, h * HEAD : (h + 1) * HEAD]
    for j in range(GROUP):
        qj[j][sh] = qs[sh * GROUP + j]
    loads[6].wait()

    near, relay = [], []

    def spread_near(j):
        take(kv[j])
        near.append(
            (
                sems.copy(kj[j].at[sw], kj[j].at[sw], after),
                sems.copy(vj[j].at[sw], vj[j].at[sw], before),
                sems.copy(kj[j].at[sw], kj[j].at[sw], before),
                sems.copy(vj[j].at[sw], vj[j].at[sw], after),
            )
        )
        done.extend(near[j])

    def spread_far(j):
        take(near[j][:2])
        left, right = turn(sw, 3, GRID), turn(sw, 1, GRID)
        relay.append(
            (
                sems.copy(kj[j].at[left], kj[j].at[left], after),
                sems.copy(vj[j].at[right], vj[j].at[right], before),
            )
        )
        done.extend(relay[j])

    def owner_at(step):
        return turn(dp, step, 16)

    kv.append(send_kv(1))
    take(mate_in)
    mate_east, mate_west = pass_on(mate, east), pass_on(mate, west)
    twin_in.append(pass_on(mate, twin))
    spread_near(0)
    q_got = [scatter(qs, qj[0].at[sh], 0)]
    kv.append(send_kv(2))
    own_east.wait_recv()
    own_far = pass_on(owner_at(12), east)
    twin_in.append(pass_on(owner_at(12), twin))
    own_west.wait_recv()
    twin_in.append(pass_on(owner_at(4), twin))
    spread_far(0)
    spread_near(1)
    q_got.append(scatter(qs, qj[1].at[sh], 1))
    q_got.append(scatter(qs, qj[2].at[sh], 2))
    mate_west.wait_recv()
    mate_far = pass_on(flip(owner_at(4), 2), west)
    twin_in.append(pass_on(flip(owner_at(4), 2), twin))
    mate_east.wait_recv()
    twin_in.append(pass_on(flip(owner_at(12), 2), twin))
    own_far.wait_recv()
    twin_in.append(pass_on(owner_at(8), twin))
    mate_far.wait_recv()
    twin_in.append(pass_on(flip(owner_at(8), 2), twin))
    spread_far(1)
    spread_near(2)
    done.extend(twin_in + mate_in + [own_east, own_west, mate_east, mate_west, own_far, mate_far])

    def window(stack, i, c):
        row, col = table[0, i, sw], table[1, i, sw]
        return stack[col + c, pl.ds(row, WINDOW)].reshape(WINDOW * TOK, HEAD)

    o_got = []

    def forward(j):
        take(near[j][2:])
        take(relay[j])
        take(q_got[j])

        def unit(i, carry):
            q = qj[j][i]
            scores = [dot(window(kj[j], i, c), q, NT) * factor for c in range(WINDOW)]
            top = functools.reduce(
                jnp.maximum, [jnp.max(s, axis=0, keepdims=True) for s in scores]
            )
            expo = [jnp.exp(s - top) for s in scores]
            total = sum(jnp.sum(e, axis=0, keepdims=True) for e in expo)
            inverse = 1.0 / total
            attended = jnp.zeros((HEAD, TOK), F32)
            for c in range(WINDOW):
                p = (expo[c] * inverse).astype(BF)
                prob[j, i, c] = p.reshape(WINDOW, TOK, TOK)
                attended = attended + dot(window(vj[j], i, c), p, TN)
            att[j, i] = attended
            oj[j][i] = attended.T.astype(BF)
            return carry

        lax.fori_loop(0, GRID, unit, 0)
        oh[sh * GROUP + j] = oj[j][sh]
        made = [sems.copy(oj[j].at[p[1]], oh.at[sh * GROUP + j], p) for p in row_peer]
        done.extend(made)
        o_got.extend(made)

    def project_back():
        take(twin_in)
        made = [[], [], []]
        for d in (1, 3, 2, 0):
            target = turn(sh, d, GRID)
            cols = pl.ds(pl.multiple_of(target * SPAN, HEAD), SPAN)
            part = dot(og[...], wt[:, cols], NN) + dot(mid[...], downt[:, cols], NN)
            part = part.astype(BF)
            for j in range(GROUP):
                piece = part[:, j * HEAD : (j + 1) * HEAD]
                if d:
                    dos[target * GROUP + j] = piece
                else:
                    doj[j][sh] = piece
            if d:
                peer = (dp, target, sw)
                made[0].append(sems.copy(dos.at[target * GROUP], doj[0].at[sh], peer))
        done.extend(made[0])
        return made

    dq_got, rs_first, rs_second, back_got = [], [], [], []

    def backward(j):
        take(do_got[j])

        def unit(i, carry):
            do = doj[j][i]
            delta = jnp.sum(att[j, i] * do.astype(F32).T, axis=0, keepdims=True)
            dq = jnp.zeros((HEAD, TOK), F32)
            for c in range(WINDOW):
                dprob = dot(window(vj[j], i, c), do, NT)
                p = prob[j, i, c].reshape(WINDOW * TOK, TOK).astype(F32)
                dscore = (p * (dprob - delta) * factor).astype(BF)
                dsl[i, c] = dscore.reshape(WINDOW, TOK, TOK)
                dq = dq + dot(window(kj[j], i, c), dscore, TN)
            dqj[j][i] = dq.T.astype(BF)
            return carry

        q_all = qj[j][...].reshape(GRID * TOK, HEAD)
        do_all = doj[j][...].reshape(GRID * TOK, HEAD)
        one, two, three = (turn(sw, d, GRID) for d in (1, 2, 3))

        def sum_columns(load, other, total):
            def column(c, carry):
                lines = []
                for r in range(GRID):
                    blocks = []
                    for i in range(GRID):
                        rr = r - table[0, i, sw]
                        cc = c - table[1, i, sw]
                        inside = (rr >= 0) & (rr < WINDOW) & (cc >= 0) & (cc < WINDOW)
                        block = load(i, jnp.clip(cc, 0, WINDOW - 1), jnp.clip(rr, 0, WINDOW - 1))
                        blocks.append(jnp.where(inside, block, jnp.zeros_like(block)))
                    lines.append(jnp.concatenate(blocks, axis=1))
                lines = jnp.concatenate(lines, axis=0)
                total[c] = dot(lines, other, NN).astype(BF).reshape(GRID, TOK, HEAD)
                return carry

            lax.fori_loop(0, GRID, column, 0)

        sum_columns(lambda i, a, b: prob[j, i, a, b], do_all, dvp[j])
        v_far = sems.copy(dvp[j].at[two], relv.at[j], before)
        v_near = sems.copy(dvp[j].at[one], nearkv.at[1, j], after)
        lax.fori_loop(0, GRID, unit, 0)
        sum_columns(lambda i, a, b: dsl[i, a, b], q_all, dkp[j])
        k_far = sems.copy(dkp[j].at[two], relk.at[j], after)
        k_near = sems.copy(dkp[j].at[three], nearkv.at[0, j], before)
        rs_first.append((k_far, v_far, k_near, v_near))
        done.extend(rs_first[j])
        dqh[sh * GROUP + j] = dqj[j][sh]
        made = [sems.copy(dqj[j].at[p[1]], dqh.at[sh * GROUP + j], p) for p in row_peer]
        done.extend(made)
        dq_got.extend(made)

    def combine(j):
        take(rs_first[j][:2])
        one, three = turn(sw, 1, GRID), turn(sw, 3, GRID)
        cmbk[j] = (relk[j].astype(F32) + dkp[j][one].astype(F32)).astype(BF)
        cmbv[j] = (relv[j].astype(F32) + dvp[j][three].astype(F32)).astype(BF)
        made = (
            sems.copy(cmbk.at[j], farkv.at[0, j], after),
            sems.copy(cmbv.at[j], farkv.at[1, j], before),
        )
        done.extend(made)
        rs_second.append(made)

    def finish(j):
        take(rs_first[j][2:])
        take(rs_second[j])
        for n, (own, total, there) in enumerate(((dkp, sumk, dkh), (dvp, sumv, dvh))):
            total[j] = (
                own[j][sw].astype(F32) + nearkv[n, j].astype(F32) + farkv[n, j].astype(F32)
            ).astype(BF)
            there[sh * GROUP + j] = total[j, sh]
            made = [sems.copy(total.at[j, p[1]], there.at[sh * GROUP + j], p) for p in row_peer]
            done.extend(made)
            back_got.extend(made)

    part = 2 * RANK // GRID

    def strip(owner):
        return pl.ds(pl.multiple_of(owner * part, part), part)

    def project(blocks):
        for n in blocks:
            block = slice(n * SPAN, (n + 1) * SPAN)
            out[:, block] = (
                dot(rows[...], wt[block, :], NT) + dot(lora, up[:, block], NN)
            ).astype(BF)

    do_got = project_back()
    forward(0)
    forward(1)
    spread_far(2)
    do_got[1] = scatter(dos, doj[1].at[sh], 1)
    backward(0)
    do_got[2] = scatter(dos, doj[2].at[sh], 2)
    forward(2)
    backward(1)
    combine(0)

    take(o_got)
    for h in range(HEADS):
        rows[:, h * HEAD : (h + 1) * HEAD] = oh[h]
    lora = dot(rows[...], downt[...], NT).astype(BF)
    ad[pl.ds(0, RANK), :] = dot(mid[...], rows[...], TN).astype(BF)
    ad[pl.ds(RANK, RANK), :] = dot(lora, og[...], TN).astype(BF)
    y_got = [sems.copy(ad.at[strip(p[2])], ry.at[n], p) for n, p in enumerate(col_peer)]
    backward(2)
    combine(1)

    take(y_got)
    summed = ad[strip(sw), :].astype(F32)
    for n in range(3):
        summed = summed + ry[n].astype(F32)
    for n in range(GRID):
        zsrc[n] = summed[:, n * SPAN : (n + 1) * SPAN].astype(BF)
    z_got = [sems.copy(zsrc.at[p[1]], rz.at[n], p) for n, p in enumerate(row_peer)]
    finish(0)
    project((0, 1))

    take(z_got)
    summed = zsrc[sh].astype(F32)
    for n in range(3):
        summed = summed + rz[n].astype(F32)
    dpsrc[...] = summed.astype(BF)
    rdp[dp] = dpsrc[...]
    d_got = [sems.copy(dpsrc, rdp.at[dp], p) for p in dp_peer]
    combine(2)
    finish(1)
    project((2, 3))

    take(d_got)
    summed = rdp[0].astype(F32)
    for n in range(1, 16):
        summed = summed + rdp[n].astype(F32)
    full[sw, sh] = summed.astype(BF)
    spot = full.at[sw, sh]
    g_got = [sems.copy(spot, spot, p) for p in row_peer]
    settle()
    finish(2)

    take(g_got)
    spot = full.at[sw]
    h_got = [sems.copy(spot, spot, p) for p in col_peer]
    take(dq_got)
    for h in range(HEADS):
        dq_out[:, h * HEAD : (h + 1) * HEAD] = dqh[h]

    settle()
    take(h_got)
    norm = TOKENS ** (-0.5)
    for c in range(GRID):
        half = down_grad if c < GRID // 2 else up_grad
        start = (c % (GRID // 2)) * part
        for r in range(GRID):
            half[start : start + part, r * SPAN : (r + 1) * SPAN] = full[c, r].astype(F32) * norm

    take(back_got)
    for h in range(HEADS):
        dk_out[:, h * HEAD : (h + 1) * HEAD] = dkh[h]
        dv_out[:, h * HEAD : (h + 1) * HEAD] = dvh[h]
    for made in done + y_got + z_got + d_got + g_got + h_got:
        made.wait_send()


def finish_kernel(*refs):
    count = len(refs) // 2
    writes = [pltpu.make_async_copy(refs[n], refs[count + n], refs[-1].at[n]) for n in range(count)]
    for copy in writes:
        copy.start()
    for copy in writes:
        copy.wait()


VM = pl.BlockSpec(memory_space=pltpu.VMEM)
SM = pl.BlockSpec(memory_space=pltpu.SMEM)
ANY = pl.BlockSpec(memory_space=pl.ANY)


def shaped(*dims, kind=BF):
    return jax.ShapeDtypeStruct(dims, kind)


def body(query, key, value, first_tile, weight, down, up, out_grad):
    shape = query.shape
    q, k, v, og = (a.reshape(TOK, FEAT) for a in (query, key, value, out_grad))
    dma = pltpu.SemaphoreType.DMA
    flat = (TOK, FEAT)
    part = 2 * RANK // GRID
    tiles = (GRID, TOK, HEAD)

    def buf(*dims, kind=BF):
        return pltpu.VMEM(dims, kind)

    def each(*dims):
        return [buf(*dims) for _ in range(GROUP)]

    results = (
        shaped(*flat), shaped(*flat), shaped(*flat), shaped(*flat),
        shaped(RANK, FEAT, kind=F32), shaped(RANK, FEAT, kind=F32),
    )
    made = pl.pallas_call(
        kernel,
        name="attend",
        out_shape=tuple(pltpu.VMEM(r.shape, r.dtype) for r in results),
        in_specs=[SM] + [ANY] * 7,
        out_specs=[VM] * 6,
        scratch_shapes=[
            buf(*flat), buf(*flat), buf(*flat), buf(*flat), buf(SHARD, FEAT), buf(RANK, FEAT), buf(RANK, FEAT),
            buf(HEADS, TOK, HEAD), buf(HEADS, TOK, HEAD), buf(HEADS, TOK, HEAD), buf(HEADS, TOK, HEAD),
            buf(FEAT, FEAT), buf(TOK, RANK),
            each(GRID, *tiles), each(GRID, *tiles), each(*tiles), each(*tiles),
            buf(GROUP, GRID, WINDOW, WINDOW, TOK, TOK), buf(GROUP, GRID, HEAD, TOK, kind=F32),
            buf(GRID, WINDOW, WINDOW, TOK, TOK), each(*tiles), each(*tiles),
            each(GRID, *tiles), each(GRID, *tiles),
            buf(GROUP, *tiles), buf(GROUP, *tiles), buf(GROUP, *tiles), buf(GROUP, *tiles),
            buf(2, GROUP, *tiles), buf(2, GROUP, *tiles), buf(GROUP, *tiles), buf(GROUP, *tiles),
            buf(HEADS, TOK, HEAD), buf(HEADS, TOK, HEAD), buf(HEADS, TOK, HEAD), buf(HEADS, TOK, HEAD),
            buf(*flat), buf(2 * RANK, FEAT), buf(3, part, FEAT), buf(GRID, part, SPAN),
            buf(3, part, SPAN), buf(part, SPAN), buf(16, part, SPAN), buf(GRID, GRID, part, SPAN),
            dma((7,)), dma((COPIES,)), dma((COPIES,)),
        ],
        compiler_params=pltpu.CompilerParams(
            collective_id=0, has_side_effects=True, vmem_limit_bytes=56 << 20
        ),
    )(first_tile, q, k, v, og, weight.T, down.T, up)
    output, dq, dk, dv, down_grad, up_grad = pl.pallas_call(
        finish_kernel,
        name="finish",
        out_shape=results,
        in_specs=[VM] * 6,
        out_specs=[ANY] * 6,
        scratch_shapes=[dma((6,))],
    )(*[pltpu.with_memory_space_constraint(m, pltpu.VMEM) for m in made])
    return (
        output.reshape(shape),
        dq.reshape(shape),
        dk.reshape(shape),
        dv.reshape(shape),
        down_grad.T,
        up_grad,
    )


def solution(mesh):
    tiles = P("dp", None, "sh", "sw", None)
    return jax.shard_map(
        body,
        mesh=mesh,
        in_specs=(tiles, tiles, tiles, P(), P(None, "dp"), P(), P(), tiles),
        out_specs=(tiles, tiles, tiles, tiles, P(), P()),
        check_vma=False,
    )
```

```python
import functools

import jax
import jax.numpy as jnp
from jax import lax
from jax.experimental import pallas as pl
from jax.experimental.pallas import tpu as pltpu
from jax.sharding import PartitionSpec as P

MESH = pl.DeviceIdType.MESH
HEADS = 12
HEAD = 128
WINDOW = 3
GROUP = 3
GRID = 4
TOK = 128
RANK = 64
FEAT = 1536
SPAN = GROUP * HEAD
SHARD = 96
TOKENS = 32768
BF = jnp.bfloat16
F32 = jnp.float32
NT = (((1,), (1,)), ((), ()))
TN = (((0,), (0,)), ((), ()))
NN = (((1,), (0,)), ((), ()))


def dot(a, b, dims):
    return lax.dot_general(a, b, dims, preferred_element_type=F32)


class Sems:
    def __init__(self, send, recv):
        self.send, self.recv, self.used = send, recv, 0

    def copy(self, src, dst, device):
        slot = self.used
        self.used += 1
        made = pltpu.make_async_remote_copy(
            src_ref=src,
            dst_ref=dst,
            send_sem=self.send.at[slot],
            recv_sem=self.recv.at[slot],
            device_id=device,
            device_id_type=MESH,
        )
        made.start()
        return made


def place():
    return lax.axis_index("dp"), lax.axis_index("sh"), lax.axis_index("sw")


def turn(index, by, size):
    return lax.rem(index + by, size)


def flip(dp, bit):
    return dp + bit - 2 * bit * lax.rem(lax.div(dp, bit), 2)


COPIES = 16 + 36 + 18 + 18 + 36 + 27


def kernel(
    table, q_hbm, k_hbm, v_hbm, og_hbm, w_hbm, down_hbm, up_hbm,
    out, dq_out, dk_out, dv_out, down_grad, up_grad,
    q_in, k_in, v_in, og, w_in, downt, up,
    qs, ks, vs, dos, wt, mid,
    kj, vj, qj, doj, prob, att, dsl, oj, dqj, dkp, dvp,
    relk, relv, cmbk, cmbv, nearkv, farkv, sumk, sumv,
    oh, dqh, dkh, dvh, rows, ad, ry, zsrc, rz, dpsrc, rdp, full,
    local, send, recv,
):
    dp, sh, sw = place()
    sems = Sems(send, recv)
    factor = HEAD ** (-0.5)
    row_peer = [(dp, turn(sh, d, GRID), sw) for d in (1, 2, 3)]
    col_peer = [(dp, sh, turn(sw, d, GRID)) for d in (1, 2, 3)]
    dp_peer = [(turn(dp, d, 16), sh, sw) for d in range(1, 16)]
    after, before = col_peer[0], col_peer[2]
    east, west = dp_peer[3], dp_peer[11]
    mate = flip(dp, 2)
    zlo = (mate, sh, sw)
    low = lax.rem(lax.div(dp, 2), 2)
    zlo_over = (mate, turn(sh, 3 + 2 * low, GRID), sw)
    twin = (flip(dp, 1), sh, sw)
    peers = row_peer + col_peer + dp_peer + [zlo_over]

    loads = []
    for n, (src, dst) in enumerate(
        ((w_hbm, w_in), (k_hbm, k_in), (v_hbm, v_in), (og_hbm, og), (up_hbm, up), (q_hbm, q_in), (down_hbm, downt))
    ):
        made = pltpu.make_async_copy(src, dst, local.at[n])
        made.start()
        loads.append(made)
    barrier = pltpu.get_barrier_semaphore()
    for device in peers:
        pl.semaphore_signal(barrier, inc=1, device_id=device, device_id_type=MESH)

    def shard_of(owner):
        return wt.at[pl.ds(pl.multiple_of(owner * SHARD, SHARD), SHARD)]

    def half_of(owner, n):
        start = pl.multiple_of(owner * SHARD + n * (SHARD // 2), SHARD // 2)
        return wt.at[pl.ds(start, SHARD // 2)]

    def pass_on(owner, peer):
        return sems.copy(shard_of(owner), shard_of(owner), peer)

    loads[0].wait()
    wt[pl.ds(pl.multiple_of(dp * SHARD, SHARD), SHARD), :] = w_in[...]
    loads[1].wait()
    loads[2].wait()

    def split_kv(j):
        for h in range(j, HEADS, GROUP):
            cols = slice(h * HEAD, (h + 1) * HEAD)
            ks[h] = k_in[:, cols]
            vs[h] = v_in[:, cols]

    split_kv(0)
    pl.semaphore_wait(barrier, len(peers))

    done = []

    def scatter(stack, dst, j):
        made = [sems.copy(stack.at[p[1] * GROUP + j], dst, p) for p in row_peer]
        done.extend(made)
        return made

    def settle():
        while done:
            done.pop().wait_send()

    def take(copies):
        for made in copies:
            made.wait_recv()

    def send_kv(j):
        return scatter(ks, kj[j].at[sw, sh], j) + scatter(vs, vj[j].at[sw, sh], j)

    kv = [send_kv(0)]
    mate_in = [
        sems.copy(half_of(dp, n), half_of(dp, n), peer) for n, peer in enumerate((zlo, zlo_over))
    ]
    own_east, own_west = pass_on(dp, east), pass_on(dp, west)
    twin_in = [pass_on(dp, twin)]
    split_kv(1)
    split_kv(2)
    for j in range(GROUP):
        kj[j][sw, sh] = ks[sh * GROUP + j]
        vj[j][sw, sh] = vs[sh * GROUP + j]
    loads[3].wait()
    loads[4].wait()
    mid[...] = dot(og[...], up[...], NT).astype(BF)
    loads[5].wait()
    for h in range(HEADS):
        qs[h] = q_in[:, h * HEAD : (h + 1) * HEAD]
    for j in range(GROUP):
        qj[j][sh] = qs[sh * GROUP + j]
    loads[6].wait()

    near, relay = [], []

    def spread_near(j):
        take(kv[j])
        near.append(
            (
                sems.copy(kj[j].at[sw], kj[j].at[sw], after),
                sems.copy(vj[j].at[sw], vj[j].at[sw], before),
                sems.copy(kj[j].at[sw], kj[j].at[sw], before),
                sems.copy(vj[j].at[sw], vj[j].at[sw], after),
            )
        )
        done.extend(near[j])

    def spread_far(j):
        take(near[j][:2])
        left, right = turn(sw, 3, GRID), turn(sw, 1, GRID)
        relay.append(
            (
                sems.copy(kj[j].at[left], kj[j].at[left], after),
                sems.copy(vj[j].at[right], vj[j].at[right], before),
            )
        )
        done.extend(relay[j])

    def owner_at(step):
        return turn(dp, step, 16)

    kv.append(send_kv(1))
    kv.append(send_kv(2))
    q_got = [scatter(qs, qj[j].at[sh], j) for j in range(GROUP)]
    take(mate_in)
    mate_east, mate_west = pass_on(mate, east), pass_on(mate, west)
    twin_in.append(pass_on(mate, twin))
    spread_near(0)
    own_east.wait_recv()
    own_far = pass_on(owner_at(12), east)
    twin_in.append(pass_on(owner_at(12), twin))
    own_west.wait_recv()
    twin_in.append(pass_on(owner_at(4), twin))
    spread_far(0)
    spread_near(1)
    mate_west.wait_recv()
    mate_far = pass_on(flip(owner_at(4), 2), west)
    twin_in.append(pass_on(flip(owner_at(4), 2), twin))
    mate_east.wait_recv()
    twin_in.append(pass_on(flip(owner_at(12), 2), twin))
    own_far.wait_recv()
    twin_in.append(pass_on(owner_at(8), twin))
    mate_far.wait_recv()
    twin_in.append(pass_on(flip(owner_at(8), 2), twin))
    spread_far(1)
    spread_near(2)
    done.extend(twin_in + mate_in + [own_east, own_west, mate_east, mate_west, own_far, mate_far])

    def window(stack, i, c):
        row, col = table[0, i, sw], table[1, i, sw]
        return stack[col + c, pl.ds(row, WINDOW)].reshape(WINDOW * TOK, HEAD)

    o_got = []

    def forward(j):
        take(near[j][2:])
        take(relay[j])
        take(q_got[j])

        def unit(i, carry):
            q = qj[j][i]
            scores = [dot(window(kj[j], i, c), q, NT) * factor for c in range(WINDOW)]
            top = functools.reduce(
                jnp.maximum, [jnp.max(s, axis=0, keepdims=True) for s in scores]
            )
            expo = [jnp.exp(s - top) for s in scores]
            total = sum(jnp.sum(e, axis=0, keepdims=True) for e in expo)
            inverse = 1.0 / total
            attended = jnp.zeros((HEAD, TOK), F32)
            for c in range(WINDOW):
                p = (expo[c] * inverse).astype(BF)
                prob[j, i, c] = p.reshape(WINDOW, TOK, TOK)
                attended = attended + dot(window(vj[j], i, c), p, TN)
            att[j, i] = attended
            oj[j][i] = attended.T.astype(BF)
            return carry

        lax.fori_loop(0, GRID, unit, 0)
        oh[sh * GROUP + j] = oj[j][sh]
        made = [sems.copy(oj[j].at[p[1]], oh.at[sh * GROUP + j], p) for p in row_peer]
        done.extend(made)
        o_got.extend(made)

    def project_back():
        take(twin_in)
        made = [[], [], []]
        for d in (1, 3, 2, 0):
            target = turn(sh, d, GRID)
            cols = pl.ds(pl.multiple_of(target * SPAN, HEAD), SPAN)
            part = dot(og[...], wt[:, cols], NN) + dot(mid[...], downt[:, cols], NN)
            part = part.astype(BF)
            for j in range(GROUP):
                piece = part[:, j * HEAD : (j + 1) * HEAD]
                if d:
                    dos[target * GROUP + j] = piece
                else:
                    doj[j][sh] = piece
            if d:
                peer = (dp, target, sw)
                made[0].append(sems.copy(dos.at[target * GROUP], doj[0].at[sh], peer))
        done.extend(made[0])
        return made

    dq_got, rs_first, rs_second, back_got = [], [], [], []

    def backward(j):
        take(do_got[j])

        def unit(i, carry):
            do = doj[j][i]
            delta = jnp.sum(att[j, i] * do.astype(F32).T, axis=0, keepdims=True)
            dq = jnp.zeros((HEAD, TOK), F32)
            for c in range(WINDOW):
                dprob = dot(window(vj[j], i, c), do, NT)
                p = prob[j, i, c].reshape(WINDOW * TOK, TOK).astype(F32)
                dscore = (p * (dprob - delta) * factor).astype(BF)
                dsl[i, c] = dscore.reshape(WINDOW, TOK, TOK)
                dq = dq + dot(window(kj[j], i, c), dscore, TN)
            dqj[j][i] = dq.T.astype(BF)
            return carry

        q_all = qj[j][...].reshape(GRID * TOK, HEAD)
        do_all = doj[j][...].reshape(GRID * TOK, HEAD)
        one, two, three = (turn(sw, d, GRID) for d in (1, 2, 3))

        def sum_columns(load, other, total):
            def column(c, carry):
                lines = []
                for r in range(GRID):
                    blocks = []
                    for i in range(GRID):
                        rr = r - table[0, i, sw]
                        cc = c - table[1, i, sw]
                        inside = (rr >= 0) & (rr < WINDOW) & (cc >= 0) & (cc < WINDOW)
                        block = load(i, jnp.clip(cc, 0, WINDOW - 1), jnp.clip(rr, 0, WINDOW - 1))
                        blocks.append(jnp.where(inside, block, jnp.zeros_like(block)))
                    lines.append(jnp.concatenate(blocks, axis=1))
                lines = jnp.concatenate(lines, axis=0)
                total[c] = dot(lines, other, NN).astype(BF).reshape(GRID, TOK, HEAD)
                return carry

            lax.fori_loop(0, GRID, column, 0)

        sum_columns(lambda i, a, b: prob[j, i, a, b], do_all, dvp[j])
        v_far = sems.copy(dvp[j].at[two], relv.at[j], before)
        v_near = sems.copy(dvp[j].at[one], nearkv.at[1, j], after)
        lax.fori_loop(0, GRID, unit, 0)
        sum_columns(lambda i, a, b: dsl[i, a, b], q_all, dkp[j])
        k_far = sems.copy(dkp[j].at[two], relk.at[j], after)
        k_near = sems.copy(dkp[j].at[three], nearkv.at[0, j], before)
        rs_first.append((k_far, v_far, k_near, v_near))
        done.extend(rs_first[j])
        dqh[sh * GROUP + j] = dqj[j][sh]
        made = [sems.copy(dqj[j].at[p[1]], dqh.at[sh * GROUP + j], p) for p in row_peer]
        done.extend(made)
        dq_got.extend(made)

    def combine(j):
        take(rs_first[j][:2])
        one, three = turn(sw, 1, GRID), turn(sw, 3, GRID)
        cmbk[j] = (relk[j].astype(F32) + dkp[j][one].astype(F32)).astype(BF)
        cmbv[j] = (relv[j].astype(F32) + dvp[j][three].astype(F32)).astype(BF)
        made = (
            sems.copy(cmbk.at[j], farkv.at[0, j], after),
            sems.copy(cmbv.at[j], farkv.at[1, j], before),
        )
        done.extend(made)
        rs_second.append(made)

    def finish(j):
        take(rs_first[j][2:])
        take(rs_second[j])
        for n, (own, total, there) in enumerate(((dkp, sumk, dkh), (dvp, sumv, dvh))):
            total[j] = (
                own[j][sw].astype(F32) + nearkv[n, j].astype(F32) + farkv[n, j].astype(F32)
            ).astype(BF)
            there[sh * GROUP + j] = total[j, sh]
            made = [sems.copy(total.at[j, p[1]], there.at[sh * GROUP + j], p) for p in row_peer]
            done.extend(made)
            back_got.extend(made)

    part = 2 * RANK // GRID

    def strip(owner):
        return pl.ds(pl.multiple_of(owner * part, part), part)

    def project(blocks):
        for n in blocks:
            block = slice(n * SPAN, (n + 1) * SPAN)
            out[:, block] = (
                dot(rows[...], wt[block, :], NT) + dot(lora, up[:, block], NN)
            ).astype(BF)

    do_got = project_back()
    forward(0)
    do_got[1] = scatter(dos, doj[1].at[sh], 1)
    forward(1)
    spread_far(2)
    do_got[2] = scatter(dos, doj[2].at[sh], 2)
    backward(0)
    forward(2)
    backward(1)
    combine(0)

    take(o_got)
    for h in range(HEADS):
        rows[:, h * HEAD : (h + 1) * HEAD] = oh[h]
    lora = dot(rows[...], downt[...], NT).astype(BF)
    ad[pl.ds(0, RANK), :] = dot(mid[...], rows[...], TN).astype(BF)
    ad[pl.ds(RANK, RANK), :] = dot(lora, og[...], TN).astype(BF)
    y_got = [sems.copy(ad.at[strip(p[2])], ry.at[n], p) for n, p in enumerate(col_peer)]
    backward(2)
    combine(1)

    take(y_got)
    summed = ad[strip(sw), :].astype(F32)
    for n in range(3):
        summed = summed + ry[n].astype(F32)
    for n in range(GRID):
        zsrc[n] = summed[:, n * SPAN : (n + 1) * SPAN].astype(BF)
    z_got = [sems.copy(zsrc.at[p[1]], rz.at[n], p) for n, p in enumerate(row_peer)]
    finish(0)
    project((0, 1))

    take(z_got)
    summed = zsrc[sh].astype(F32)
    for n in range(3):
        summed = summed + rz[n].astype(F32)
    dpsrc[...] = summed.astype(BF)
    rdp[dp] = dpsrc[...]
    d_got = [sems.copy(dpsrc, rdp.at[dp], p) for p in dp_peer]
    combine(2)
    finish(1)
    project((2, 3))

    take(d_got)
    summed = rdp[0].astype(F32)
    for n in range(1, 16):
        summed = summed + rdp[n].astype(F32)
    full[sw, sh] = summed.astype(BF)
    spot = full.at[sw, sh]
    g_got = [sems.copy(spot, spot, p) for p in row_peer]
    settle()
    finish(2)

    take(g_got)
    spot = full.at[sw]
    h_got = [sems.copy(spot, spot, p) for p in col_peer]
    take(dq_got)
    for h in range(HEADS):
        dq_out[:, h * HEAD : (h + 1) * HEAD] = dqh[h]

    settle()
    take(h_got)
    norm = TOKENS ** (-0.5)
    for c in range(GRID):
        half = down_grad if c < GRID // 2 else up_grad
        start = (c % (GRID // 2)) * part
        for r in range(GRID):
            half[start : start + part, r * SPAN : (r + 1) * SPAN] = full[c, r].astype(F32) * norm

    take(back_got)
    for h in range(HEADS):
        dk_out[:, h * HEAD : (h + 1) * HEAD] = dkh[h]
        dv_out[:, h * HEAD : (h + 1) * HEAD] = dvh[h]
    for made in done + y_got + z_got + d_got + g_got + h_got:
        made.wait_send()


def finish_kernel(*refs):
    count = len(refs) // 2
    writes = [pltpu.make_async_copy(refs[n], refs[count + n], refs[-1].at[n]) for n in range(count)]
    for copy in writes:
        copy.start()
    for copy in writes:
        copy.wait()


VM = pl.BlockSpec(memory_space=pltpu.VMEM)
SM = pl.BlockSpec(memory_space=pltpu.SMEM)
ANY = pl.BlockSpec(memory_space=pl.ANY)


def shaped(*dims, kind=BF):
    return jax.ShapeDtypeStruct(dims, kind)


def body(query, key, value, first_tile, weight, down, up, out_grad):
    shape = query.shape
    q, k, v, og = (a.reshape(TOK, FEAT) for a in (query, key, value, out_grad))
    dma = pltpu.SemaphoreType.DMA
    flat = (TOK, FEAT)
    part = 2 * RANK // GRID
    tiles = (GRID, TOK, HEAD)

    def buf(*dims, kind=BF):
        return pltpu.VMEM(dims, kind)

    def each(*dims):
        return [buf(*dims) for _ in range(GROUP)]

    results = (
        shaped(*flat), shaped(*flat), shaped(*flat), shaped(*flat),
        shaped(RANK, FEAT, kind=F32), shaped(RANK, FEAT, kind=F32),
    )
    made = pl.pallas_call(
        kernel,
        name="attend",
        out_shape=tuple(pltpu.VMEM(r.shape, r.dtype) for r in results),
        in_specs=[SM] + [ANY] * 7,
        out_specs=[VM] * 6,
        scratch_shapes=[
            buf(*flat), buf(*flat), buf(*flat), buf(*flat), buf(SHARD, FEAT), buf(RANK, FEAT), buf(RANK, FEAT),
            buf(HEADS, TOK, HEAD), buf(HEADS, TOK, HEAD), buf(HEADS, TOK, HEAD), buf(HEADS, TOK, HEAD),
            buf(FEAT, FEAT), buf(TOK, RANK),
            each(GRID, *tiles), each(GRID, *tiles), each(*tiles), each(*tiles),
            buf(GROUP, GRID, WINDOW, WINDOW, TOK, TOK), buf(GROUP, GRID, HEAD, TOK, kind=F32),
            buf(GRID, WINDOW, WINDOW, TOK, TOK), each(*tiles), each(*tiles),
            each(GRID, *tiles), each(GRID, *tiles),
            buf(GROUP, *tiles), buf(GROUP, *tiles), buf(GROUP, *tiles), buf(GROUP, *tiles),
            buf(2, GROUP, *tiles), buf(2, GROUP, *tiles), buf(GROUP, *tiles), buf(GROUP, *tiles),
            buf(HEADS, TOK, HEAD), buf(HEADS, TOK, HEAD), buf(HEADS, TOK, HEAD), buf(HEADS, TOK, HEAD),
            buf(*flat), buf(2 * RANK, FEAT), buf(3, part, FEAT), buf(GRID, part, SPAN),
            buf(3, part, SPAN), buf(part, SPAN), buf(16, part, SPAN), buf(GRID, GRID, part, SPAN),
            dma((7,)), dma((COPIES,)), dma((COPIES,)),
        ],
        compiler_params=pltpu.CompilerParams(
            collective_id=0, has_side_effects=True, vmem_limit_bytes=56 << 20
        ),
    )(first_tile, q, k, v, og, weight.T, down.T, up)
    output, dq, dk, dv, down_grad, up_grad = pl.pallas_call(
        finish_kernel,
        name="finish",
        out_shape=results,
        in_specs=[VM] * 6,
        out_specs=[ANY] * 6,
        scratch_shapes=[dma((6,))],
    )(*[pltpu.with_memory_space_constraint(m, pltpu.VMEM) for m in made])
    return (
        output.reshape(shape),
        dq.reshape(shape),
        dk.reshape(shape),
        dv.reshape(shape),
        down_grad.T,
        up_grad,
    )


def solution(mesh):
    tiles = P("dp", None, "sh", "sw", None)
    return jax.shard_map(
        body,
        mesh=mesh,
        in_specs=(tiles, tiles, tiles, P(), P(None, "dp"), P(), P(), tiles),
        out_specs=(tiles, tiles, tiles, tiles, P(), P()),
        check_vma=False,
    )
```
